128 devices in a mesh: ea: 32 (over z, x_lo, y), row: 4 (over x_hi, core).
Axes of the slice: x: 4 (x_hi: 2, x_lo: 2; x = x_hi * 2 + x_lo), y: 4, z: 4, core: 2. Of those that a mesh axis runs over, the one named last changes fastest.
Arguments:
- image_tokens: bfloat16 [25216, 768], P(('ea', 'row')), may hold values from -6 to 6
- cotangent: bfloat16 [25216, 768], P(('ea', 'row')), may hold values from -6 to 6
- routes: int32 [2, 25216, 2], P(None, ('ea', 'row')), may hold values from 0 to 31, all different within a row; in each aligned block of 197 rows (0 to 196, 197 to 393, ..., all dimensions but the last counted through in order) at most 13 rows name the same one
- norm_gains: bfloat16 [2, 2, 768], P(None, None, 'ea'), may hold values from 0.099609375 to 1.8984375
- norm_biases: bfloat16 [2, 2, 768], P(None, None, 'ea'), may hold values from -4 to 4
- qkv_weight: bfloat16 [2, 768, 2304], P(None, 'ea'), may hold values from -0.21875 to 0.21875
- out_weight: bfloat16 [2, 768, 768], P(None, 'ea'), may hold values from -0.875 to 0.875
- router_weight: bfloat16 [2, 768, 32], P(None, 'ea'), may hold values from -0.15625 to 0.15625
- expert_in: bfloat16 [2, 32, 768, 3072], P(None, 'ea', None, 'row'), may hold values from -0.21875 to 0.21875
- expert_out: bfloat16 [2, 32, 3072, 768], P(None, 'ea', 'row'), may hold values from -2 to 2
Outputs:
- block_out: bfloat16 [25216, 768], P(('ea', 'row'))
- input_grad: float32 [25216, 768], P(('ea', 'row'))
- gains_grad: float32 [2, 2, 768], P(None, None, 'ea')
- biases_grad: float32 [2, 2, 768], P(None, None, 'ea')
- qkv_grad: float32 [2, 768, 2304], P(None, 'ea')
- out_grad: float32 [2, 768, 768], P(None, 'ea')
- router_grad: float32 [2, 768, 32], P(None, 'ea')
- expert_in_grad: float32 [2, 32, 768, 3072], P(None, 'ea', None, 'row')
- expert_out_grad: float32 [2, 32, 3072, 768], P(None, 'ea', 'row')
The draws below stay inside these ranges and needn't reach their ends.
Inputs may be any that keep to these rules, and one draw needn't show every extreme that they name: `routes`: in each block, among the 197 tokens of one device (aligned blocks of rows), no expert is named more than 13 times, and a token's two experts differ.
All inputs are finite; a program needn't handle non-finite values.
Results may differ from the reference program's by a relative error of at most 0.03.
Values may be sent and summed in bfloat16 or wider, within the bound.
No kernel may reach another device: no remote copies, remote signals or barrier semaphores. Data moves between devices by JAX's collectives and lax.ppermute only.
A program may use at most 192 MiB of HBM per device.

```python
import math
import jax
import jax.numpy as jnp
import numpy as np
from jax import lax

D = 768
HEADS = 12
HEAD = 64
FF = 3072
SEQ = 197
LAYERS = 2
EXPERTS = 32
T_DEV = 197
IMAGES = 128
TOKENS = 25216
CAP = 13
N_EA = 32
N_ROW = 4


def shard_levels(key, dims, shards, low, high):
    def one(axis_at, blocks):
        steps = jax.random.uniform(jax.random.fold_in(jax.random.fold_in(key, 6), axis_at), (blocks,), jnp.float32, low / len(shards), high / len(shards))
        return jnp.repeat(jnp.exp(steps), dims[axis_at] // blocks).reshape((-1,) + (1,) * (len(dims) - axis_at - 1))

    level = one(*shards[0])
    for cut in shards[1:]:
        level = level * one(*cut)
    return level


def shared_out(own_key, own, number, rows, amount, top, most, skew):
    sequence = jax.random.permutation(own_key, amount)
    heavy_load, usual = load_shares(amount, rows * top, most, skew, True), load_shares(amount, rows * top, most, skew, False)
    places = jnp.arange(amount)

    def named(lengths, offset_by):
        used = int((lengths > 0).sum())
        fixed = max(1, used // 4)
        moved = fixed + (places - fixed + offset_by * (used - fixed)) % max(1, amount - fixed)
        return jnp.zeros((amount,), jnp.int32).at[sequence[jnp.where(places < fixed, places, moved)]].set(jnp.asarray(lengths, jnp.int32))

    lengths = jnp.where(number % 4 == 0, named(heavy_load, number // 4), named(usual, number - number // 4 - 1))
    mixed = jax.random.permutation(jax.random.fold_in(own, 3), amount)
    source_of, taker = mixed[0:amount // 2 * 2:2], mixed[1:amount // 2 * 2:2]
    slack = jnp.minimum(lengths[source_of] - 1, most - lengths[taker]) // 2
    slack = jnp.where((source_of == sequence[0]) | (taker == sequence[0]) | (lengths[taker] == 0), 0, jnp.maximum(slack, 0))
    moved = jax.random.randint(jax.random.fold_in(own, 4), (amount // 2,), 0, 1 << 20) % (slack + 1)
    lengths = lengths.at[source_of].add(-moved).at[taker].add(moved)
    items = jnp.searchsorted(jnp.cumsum(lengths), jnp.arange(rows * top), side="right").astype(jnp.int32)
    listing = items.reshape(top, rows).T
    listing = listing[jax.random.permutation(jax.random.fold_in(own, 1), rows)]
    offset_by = jax.random.randint(jax.random.fold_in(own, 2), (rows, 1), 0, top)
    return jnp.take_along_axis(listing, (jnp.arange(top)[None, :] + offset_by) % top, axis=1)


def load_shares(amount, total, limit, slope, full):
    portions = [(1 << 20) // math.isqrt(standing ** slope) + 1 for standing in range(1, amount + 1)]
    largest = limit if full else min(limit, max(-(-total // amount), total * portions[0] // sum(portions)))
    least = 1 if total - largest >= amount - 1 else 0
    counts, spare = [largest] + [least] * (amount - 1), total - largest - least * (amount - 1)
    while spare > 0:
        free = [i for i in range(1, amount) if counts[i] < largest] or [i for i in range(1, amount) if counts[i] < limit]
        mass, budget = sum([portions[i] for i in free]), spare
        for i in free:
            more = min(limit - counts[i], max(1, budget * portions[i] // mass), spare)
            counts[i] = counts[i] + more
            spare = spare - more
    return np.array(counts)


def bell_draw(rng, dims, scale, reach, split=(), kind=jnp.bfloat16):
    factor_of = shard_levels(rng, dims, split, -0.22, 0.18) if split else 1.0
    array = jax.random.normal(rng, dims, jnp.float32) * scale * factor_of
    return jnp.minimum(jnp.maximum(array, -reach), reach).astype(kind)


def setup_inputs(seed: int = 0) -> dict:
    splits = jax.random.split(jax.random.key(seed), 11)
    image_tokens = bell_draw(splits[0], (TOKENS, D), 1.0, 6.0, ((0, 128),))
    cotangent = bell_draw(splits[1], (TOKENS, D), 1.0, 6.0, ((0, 128),))
    routes_keys = jax.random.split(jax.random.fold_in(splits[2], 1), LAYERS * TOKENS // T_DEV)
    routes_turns = jax.random.permutation(jax.random.fold_in(splits[2], 3), LAYERS * TOKENS // T_DEV)
    routes = jax.vmap(lambda own, number: shared_out(jax.random.fold_in(splits[2], 2), own, number, T_DEV, EXPERTS, 2, CAP, 1))(routes_keys, routes_turns).reshape((LAYERS, TOKENS, 2))
    norm_gains = jnp.clip(1.0 + 0.18 * jax.random.normal(splits[3], (LAYERS, 2, D), jnp.float32), 0.099609375, 1.8984375).astype(jnp.bfloat16)
    norm_biases = bell_draw(splits[4], (LAYERS, 2, D), 0.3, 4.0, ((2, 32),))
    qkv_weight = bell_draw(splits[5], (LAYERS, D, 3 * D), D ** -0.5, 0.21875, ((1, 32),))
    out_weight = bell_draw(splits[6], (LAYERS, D, D), (D // 16) ** -0.5, 0.875, ((1, 32),))
    router_weight = bell_draw(splits[7], (LAYERS, D, EXPERTS), (2 * D) ** -0.5, 0.15625, ((1, 32),))
    expert_in = bell_draw(splits[8], (LAYERS, EXPERTS, D, FF), D ** -0.5, 0.21875, ((1, 32), (3, 4)))
    expert_out = bell_draw(splits[9], (LAYERS, EXPERTS, FF, D), (FF // 512 + 1) ** -0.5, 2.0, ((1, 32), (2, 4)))
    return {"image_tokens": image_tokens, "cotangent": cotangent, "routes": routes, "norm_gains": norm_gains, "norm_biases": norm_biases, "qkv_weight": qkv_weight, "out_weight": out_weight, "router_weight": router_weight, "expert_in": expert_in, "expert_out": expert_out}


EPS = 1e-06
HIGH = lax.Precision.HIGHEST

@jax.custom_vjp
def low(v):
    return lax.optimization_barrier(v.astype(jnp.bfloat16)).astype(jnp.float32)

@jax.custom_vjp
def low_back(v):
    return v

def low_keep(v):
    return (low(v), None)

def low_pass(kept, grad):
    return (grad,)

def back_keep(v):
    return (v, None)

def back_low(kept, grad):
    return (low(grad),)
low.defvjp(low_keep, low_pass)
low_back.defvjp(back_keep, back_low)

def layer_norm(values, gain, bias):
    center = lax.optimization_barrier(jnp.mean(values, axis=-1, keepdims=True))
    shifted = values - center
    spread = lax.optimization_barrier(jnp.mean(shifted * shifted, axis=-1, keepdims=True))
    return shifted * lax.rsqrt(spread + EPS) * gain + bias

def attend(group_rows, gain, bias, qkv_w, out_w):
    count = group_rows.shape[0]
    normed = low(layer_norm(group_rows, gain, bias))
    projected = low_back(jnp.einsum('gsd,de->gse', normed, qkv_w, precision=HIGH))
    projected = low(projected).reshape(count, SEQ, 3, HEADS, HEAD)
    query = projected[:, :, 0]
    key_part = projected[:, :, 1]
    value_part = projected[:, :, 2]
    raw_scores = low_back(jnp.einsum('gqhd,gkhd->ghqk', query, key_part, precision=HIGH))
    shares = jax.nn.softmax(raw_scores * HEAD ** (-0.5), axis=-1)
    mixed = jnp.einsum('ghqk,gkhd->gqhd', low(shares), value_part, precision=HIGH)
    mixed = low(mixed.reshape(count, SEQ, HEADS * HEAD))
    return group_rows + low_back(jnp.einsum('gsd,de->gse', mixed, out_w, precision=HIGH))

def expert_ffn(operands):
    rows, w_in, w_out = operands
    pre_act = low_back(jnp.dot(rows, w_in, precision=HIGH))
    hidden = low(jax.nn.gelu(pre_act, approximate=False))
    return low(low_back(jnp.dot(hidden, w_out, precision=HIGH)))

def slot_rows(chosen):
    devices = N_EA * N_ROW
    per_device = chosen.reshape(devices, 2 * T_DEV)
    onehot = (per_device[..., None] == jnp.arange(EXPERTS, dtype=jnp.int32)).astype(jnp.int32)
    before = jnp.cumsum(onehot, axis=1) - onehot
    position = lax.optimization_barrier(jnp.sum(before * onehot, axis=-1)).astype(jnp.int32)
    device_ids = jnp.arange(devices, dtype=jnp.int32)[:, None]
    flat = per_device * (devices * CAP) + device_ids * CAP + position
    return flat.reshape(-1).astype(jnp.int32)

def mix_experts(after_attn, gain, bias, router_w, w_in, w_out, chosen):
    slot_count = N_EA * N_ROW * CAP
    normed = low(layer_norm(after_attn, gain, bias))
    router = jax.nn.softmax(jnp.dot(normed, router_w, precision=HIGH), axis=-1)
    gates = jnp.take_along_axis(router, chosen, axis=1)
    index = slot_rows(chosen)
    paired = jnp.repeat(normed, 2, axis=0)
    buffer = jnp.zeros((EXPERTS * slot_count, D), jnp.float32).at[index].set(paired)
    buffer = low_back(buffer.reshape(EXPERTS, slot_count, D))
    results = lax.map(jax.checkpoint(expert_ffn), (buffer, w_in, w_out))
    picked = results.reshape(EXPERTS * slot_count, D)[index].reshape(TOKENS, 2, D)
    return after_attn + lax.optimization_barrier(jnp.sum(gates[..., None] * picked, axis=1))

def reference(image_tokens, cotangent, routes, norm_gains, norm_biases, qkv_weight, out_weight, router_weight, expert_in, expert_out):
    per_group = math.gcd(IMAGES, 16)

    def forward(state, gains, biases, qkv_w, out_w, router_w, w_in, w_out):
        for depth in range(LAYERS):
            grouped = state.reshape(IMAGES // per_group, per_group, SEQ, D)

            def one_group(group_rows, depth=depth):
                return attend(group_rows, gains[depth, 0], biases[depth, 0], qkv_w[depth], out_w[depth])
            after_attn = lax.map(jax.checkpoint(one_group), grouped).reshape(TOKENS, D)
            state = mix_experts(after_attn, gains[depth, 1], biases[depth, 1], router_w[depth], w_in[depth], w_out[depth], routes[depth])
        return state
    floats = (image_tokens, norm_gains, norm_biases, qkv_weight, out_weight, router_weight, expert_in, expert_out)
    floats = tuple((item.astype(jnp.float32) for item in floats))
    result, pull = jax.vjp(forward, *floats)
    grads = pull(cotangent.astype(jnp.float32))
    return (result.astype(jnp.bfloat16), grads[0], grads[1], grads[2], grads[3], grads[4], grads[5], grads[6], grads[7])
```

```python
import jax
import jax.numpy as jnp
from jax import lax
from jax.sharding import Mesh
from jax.sharding import PartitionSpec as P

HEADS = 12
HEAD = 64
SEQ = 197
LAYERS = 2
EPS = 1e-06
HIGH = lax.Precision.HIGHEST
BF = jnp.bfloat16
F32 = jnp.float32
SLOTS = 16
SCALE = HEAD ** (-0.5)
GROUP = ("ea", "half")


def dot(a, b, dims=((1,), (0,))):
    return lax.dot_general(a, b, (dims, ((), ())), preferred_element_type=F32)


def dot_nt(a, b):
    return dot(a, b, ((1,), (1,)))


def dot_tn(a, b):
    return dot(a, b, ((0,), (0,)))


def swap_core(value):
    return lax.ppermute(value, "core", [(0, 1), (1, 0)])


def swap_half(value):
    return lax.ppermute(value, "half", [(0, 1), (1, 0)])


def exchange(rows):
    return lax.all_to_all(rows, GROUP, split_axis=0, concat_axis=0, tiled=True)


def gelu_parts(x):
    mag = jnp.abs(x)
    t = 1.0 / (1.0 + (0.3275911 * 0.7071067811865476) * mag)
    bell = jnp.exp(-0.5 * x * x)
    poly = 0.5 * t * (
        0.254829592
        + t * (-0.284496736 + t * (1.421413741 + t * (-1.453152027 + t * 1.061405429)))
    )
    tail = poly * bell
    cdf = jnp.where(x < 0, tail, 1.0 - tail)
    return cdf, cdf + x * bell * 0.3989422804014327


def normalize(x, gain, bias):
    center = jnp.mean(x, axis=-1, keepdims=True)
    shifted = x - center
    spread = jnp.mean(shifted * shifted, axis=-1, keepdims=True)
    inv = lax.rsqrt(spread + EPS)
    unit = shifted * inv
    return unit * gain + bias, unit, inv


def normalize_back(grad, unit, inv, gain):
    scaled = grad * gain
    mean_a = jnp.mean(scaled, axis=-1, keepdims=True)
    mean_b = jnp.mean(scaled * unit, axis=-1, keepdims=True)
    return (
        inv * (scaled - mean_a - unit * mean_b),
        jnp.sum(grad * unit, axis=0),
        jnp.sum(grad, axis=0),
    )


def heads_of(matrix):
    return matrix.reshape(SEQ, HEADS, HEAD)


def gather_cols(mine):
    n = mine.shape[1]
    groups = lax.axis_size("ea")
    sent = jnp.broadcast_to(mine[None], (groups,) + mine.shape)
    got = lax.all_to_all(sent, "ea", split_axis=0, concat_axis=0).reshape(-1, n)
    other = swap_core(got)
    first = lax.axis_index("core") == 0
    return jnp.where(first, got, other), jnp.where(first, other, got)


def core_cols(packed):
    n = packed.shape[1] // 2
    return lax.dynamic_slice_in_dim(packed, lax.axis_index("core") * n, n, 1)


def sum_cols(packed):
    n = packed.shape[1] // 2
    packed = packed.astype(BF)
    core = lax.axis_index("core")
    own = lax.dynamic_slice_in_dim(packed, core * n, n, 1)
    give = lax.dynamic_slice_in_dim(packed, (1 - core) * n, n, 1)
    pair = (own.astype(F32) + swap_core(give).astype(F32)).astype(BF)
    groups = lax.axis_size("ea")
    parts = lax.all_to_all(
        pair.reshape(groups, -1, n), "ea", split_axis=0, concat_axis=0
    )
    part = jnp.sum(parts.astype(F32), axis=0)
    full = part + swap_half(part)
    other = swap_core(full)
    first = core == 0
    return jnp.concatenate(
        [jnp.where(first, full, other), jnp.where(first, other, full)], axis=1
    )


def pad_cols(value, cols):
    return jnp.pad(value, ((0, 0), (0, cols - value.shape[1])))


def attention(state, dense):
    qkv_w, out_w, _, gains, biases = dense
    normed, unit, inv = normalize(state, gains[0], biases[0])
    normed = normed.astype(BF)
    projected = dot(normed, qkv_w).astype(BF)
    query, key_part, value_part = (
        heads_of(projected[:, i * 768 : (i + 1) * 768]) for i in range(3)
    )
    scaled = jnp.einsum("qhd,khd->hqk", query, key_part, preferred_element_type=F32) * SCALE
    peak = jnp.max(scaled, axis=-1, keepdims=True)
    expo = jnp.exp(scaled - peak)
    total = jnp.sum(expo, axis=-1, keepdims=True)
    log_total = peak + jnp.log(total)
    shares = (expo / total).astype(BF)
    mixed = jnp.einsum("hqk,khd->qhd", shares, value_part, preferred_element_type=F32)
    mixed = mixed.reshape(state.shape).astype(BF)
    after = state + dot(mixed, out_w)
    return after, (unit, inv, normed, projected, log_total, mixed)


def attention_back(grad_after, kept, dense):
    unit, inv, normed, projected, log_total, mixed = kept
    qkv_w, out_w, _, gains, _ = dense
    tokens, width = grad_after.shape
    grad_attn = grad_after.astype(BF)
    grad_out_w = dot_tn(mixed, grad_attn)
    grad_mixed = heads_of(dot_nt(grad_attn, out_w).astype(BF))
    query, key_part, value_part = (
        heads_of(projected[:, i * width : (i + 1) * width]) for i in range(3)
    )
    scaled = jnp.einsum("qhd,khd->hqk", query, key_part, preferred_element_type=F32) * SCALE
    shares = jnp.exp(scaled - log_total)
    grad_value = jnp.einsum(
        "hqk,qhd->khd", shares.astype(BF), grad_mixed, preferred_element_type=F32
    )
    grad_shares = jnp.einsum("qhd,khd->hqk", grad_mixed, value_part, preferred_element_type=F32)
    grad_scores = shares * (grad_shares - jnp.sum(grad_shares * shares, axis=-1, keepdims=True))
    grad_raw = (grad_scores * SCALE).astype(BF)
    grad_query = jnp.einsum("hqk,khd->qhd", grad_raw, key_part, preferred_element_type=F32)
    grad_key = jnp.einsum("hqk,qhd->khd", grad_raw, query, preferred_element_type=F32)
    grad_projected = jnp.concatenate(
        [part.reshape(tokens, width) for part in (grad_query, grad_key, grad_value)], axis=1
    ).astype(BF)
    grad_qkv = dot_tn(normed, grad_projected)
    grad_normed = dot_nt(grad_projected, qkv_w)
    part_one, gain_one, bias_one = normalize_back(grad_normed, unit, inv, gains[0])
    return grad_after + part_one, grad_qkv, grad_out_w, gain_one, bias_one


def routing(chosen, experts):
    tokens = chosen.shape[0]
    flat = jnp.concatenate([chosen[:, 0], chosen[:, 1]])
    onehot = flat[:, None] == jnp.arange(experts, dtype=jnp.int32)[None, :]
    pairs = 2 * tokens
    earlier = (
        lax.broadcasted_iota(jnp.int32, (pairs, pairs), 1)
        < lax.broadcasted_iota(jnp.int32, (pairs, pairs), 0)
    ).astype(BF)
    onehot = onehot.astype(F32)
    before = dot(earlier, onehot.astype(BF))
    position = jnp.sum(before * onehot, axis=1).astype(jnp.int32)
    code = flat * (2 * SLOTS) + position
    slots = experts * 2 * SLOTS
    row_code = lax.broadcasted_iota(jnp.int32, (slots, pairs), 0)
    row_code = row_code - (row_code & SLOTS)
    send = (row_code == code[None, :]).astype(BF)
    col_code = lax.broadcasted_iota(jnp.int32, (pairs, slots), 1)
    col_code = col_code - (col_code & SLOTS)
    fetch = (col_code == code[:, None]).astype(BF)
    return onehot, send, fetch


def router_forward(normed_two, router_w, onehot):
    router = jax.nn.softmax(dot(normed_two, router_w), axis=-1)
    tokens = router.shape[0]
    gate = [
        jnp.sum(onehot[j * tokens : (j + 1) * tokens] * router, axis=1, keepdims=True)
        for j in range(2)
    ]
    return router, gate


def router_back(grad, picked, router, onehot, normed_two, router_w):
    tokens = router.shape[0]
    grad_router = 0.0
    for j in range(2):
        part = jnp.sum(grad * picked[j], axis=1, keepdims=True)
        grad_router = grad_router + onehot[j * tokens : (j + 1) * tokens] * part
    grad_logit = router * (grad_router - jnp.sum(grad_router * router, axis=-1, keepdims=True))
    grad_normed = jnp.dot(grad_logit, router_w.astype(F32).T, precision=HIGH)
    grad_router_w = jnp.dot(normed_two.astype(F32).T, grad_logit, precision=HIGH)
    return grad_normed, grad_router_w


def pack_grads(grad_qkv, grad_out_w, grad_router_w, gain_grads, bias_grads):
    small = jnp.concatenate([grad_router_w, jnp.stack(gain_grads + bias_grads, axis=1)], axis=1)
    return jnp.concatenate([grad_qkv, grad_out_w, pad_cols(small, 256)], axis=1)


def per_device(
    image_tokens,
    cotangent,
    routes,
    norm_gains,
    norm_biases,
    qkv_weight,
    out_weight,
    router_weight,
    expert_in,
    expert_out,
):
    tokens, width = image_tokens.shape
    experts = lax.axis_size("ea")
    dense = []
    small = [
        pad_cols(
            jnp.concatenate([router_weight[b], norm_gains[b].T, norm_biases[b].T], axis=1), 256
        )
        for b in range(LAYERS)
    ]
    for b in range(LAYERS):
        packed = jnp.concatenate([qkv_weight[b], out_weight[b], small[b]], axis=1)
        whole = jnp.concatenate(gather_cols(core_cols(packed)), axis=1)
        rest = whole[:, 3072:]
        gains = rest[:, experts : experts + 2].astype(F32).T
        biases = rest[:, experts + 2 : experts + 4].astype(F32).T
        dense.append((whole[:, :2304], whole[:, 2304:3072], rest[:, :experts], gains, biases))
    routed = [routing(routes[b], experts) for b in range(LAYERS)]
    w_in = [expert_in[b, 0] for b in range(LAYERS)]
    w_out = [expert_out[b, 0] for b in range(LAYERS)]

    state = image_tokens.astype(F32)
    after0, kept0 = attention(state, dense[0])
    onehot, send, fetch = routed[0]
    wide, unit0, inv0 = normalize(after0, dense[0][3][1], dense[0][4][1])
    normed0 = wide.astype(BF)
    router0, gate0 = router_forward(normed0, dense[0][2], onehot)
    arrived = exchange(dot(send[:, :tokens] + send[:, tokens:], normed0).astype(BF))
    rows0 = jnp.concatenate([arrived, swap_core(arrived)], axis=0)
    pre = dot(rows0, w_in[0])
    cdf, slope0 = gelu_parts(pre)
    hidden0 = (pre * cdf).astype(BF)
    part = dot(hidden0, w_out[0])
    half_rows = part.shape[0] // 2
    back = part[:half_rows] + swap_core(part[half_rows:].astype(BF)).astype(F32)
    returned = exchange(back.astype(BF))
    picked = dot(fetch, returned)
    picked0 = (picked[:tokens], picked[tokens:])
    state1 = after0 + gate0[0] * picked0[0] + gate0[1] * picked0[1]

    grad = cotangent.astype(F32)
    after1, kept1 = attention(state1, dense[1])
    onehot1, send1, fetch1 = routed[1]
    wide, unit1, inv1 = normalize(after1, dense[1][3][1], dense[1][4][1])
    normed1 = wide.astype(BF)
    router1, gate1 = router_forward(normed1, dense[1][2], onehot1)
    rows = dot(send1[:, :tokens] + send1[:, tokens:], normed1).astype(BF)
    grad_rows = jnp.concatenate([(g * grad).astype(BF) for g in gate1], axis=0)
    grad_rows = dot(send1, grad_rows).astype(BF)
    arrived = exchange(jnp.concatenate([rows, grad_rows], axis=1))
    both = jnp.concatenate([arrived, swap_core(arrived)], axis=0)
    rows1, grows1 = both[:, :width], both[:, width:]
    pre = dot(rows1, w_in[1])
    cdf, slope = gelu_parts(pre)
    hidden1 = (pre * cdf).astype(BF)
    grad_pre1 = (dot_nt(grows1, w_out[1]) * slope).astype(BF)
    part = jnp.concatenate([dot(hidden1, w_out[1]), dot_nt(grad_pre1, w_in[1])], axis=1)
    back = part[:half_rows] + swap_core(part[half_rows:].astype(BF)).astype(F32)
    returned = exchange(back.astype(BF))
    picked = dot(fetch1, returned)
    picked1 = (picked[:tokens, :width], picked[tokens:, :width])
    grad_sent = picked[:tokens, width:] + picked[tokens:, width:]
    block_out = (after1 + gate1[0] * picked1[0] + gate1[1] * picked1[1]).astype(BF)
    grad_w_out1 = dot_tn(hidden1, grows1)
    grad_w_in1 = dot_tn(rows1, grad_pre1)

    extra, grad_router_w1 = router_back(grad, picked1, router1, onehot1, normed1, dense[1][2])
    part_two, gain_two, bias_two = normalize_back(
        grad_sent + extra, unit1, inv1, dense[1][3][1]
    )
    grad, grad_qkv, grad_out_w, gain_one, bias_one = attention_back(
        grad + part_two, kept1, dense[1]
    )
    sums1 = sum_cols(
        pack_grads(grad_qkv, grad_out_w, grad_router_w1, [gain_one, gain_two], [bias_one, bias_two])
    )

    grad_rows = jnp.concatenate([(g * grad).astype(BF) for g in gate0], axis=0)
    arrived = exchange(dot(send, grad_rows).astype(BF))
    grows0 = jnp.concatenate([arrived, swap_core(arrived)], axis=0)
    grad_pre0 = (dot_nt(grows0, w_out[0]) * slope0).astype(BF)
    part = dot_nt(grad_pre0, w_in[0])
    back = part[:half_rows] + swap_core(part[half_rows:].astype(BF)).astype(F32)
    returned = exchange(back.astype(BF))
    picked = dot(fetch, returned)
    grad_sent = picked[:tokens] + picked[tokens:]
    grad_w_out0 = dot_tn(hidden0, grows0)
    grad_w_in0 = dot_tn(rows0, grad_pre0)
    extra, grad_router_w0 = router_back(grad, picked0, router0, onehot, normed0, dense[0][2])
    part_two, gain_two, bias_two = normalize_back(
        grad_sent + extra, unit0, inv0, dense[0][3][1]
    )
    grad, grad_qkv, grad_out_w, gain_one, bias_one = attention_back(
        grad + part_two, kept0, dense[0]
    )
    sums0 = sum_cols(
        pack_grads(grad_qkv, grad_out_w, grad_router_w0, [gain_one, gain_two], [bias_one, bias_two])
    )

    sums = jnp.stack([sums0, sums1])
    rest = sums[:, :, 3072:]
    return (
        block_out,
        grad,
        rest[:, :, experts : experts + 2].transpose(0, 2, 1),
        rest[:, :, experts + 2 : experts + 4].transpose(0, 2, 1),
        sums[:, :, :2304],
        sums[:, :, 2304:3072],
        rest[:, :, :experts],
        jnp.stack([grad_w_in0, grad_w_in1])[:, None],
        jnp.stack([grad_w_out0, grad_w_out1])[:, None],
    )


def solution(mesh):
    fine = Mesh(
        mesh.devices.reshape(mesh.shape["ea"], mesh.shape["row"] // 2, 2), ("ea", "half", "core")
    )
    row = ("half", "core")
    every = ("ea",) + row
    in_specs = (
        P(every, None),
        P(every, None),
        P(None, every, None),
        P(None, None, "ea"),
        P(None, None, "ea"),
        P(None, "ea", None),
        P(None, "ea", None),
        P(None, "ea", None),
        P(None, "ea", None, row),
        P(None, "ea", row, None),
    )
    out_specs = (
        P(every, None),
        P(every, None),
        P(None, None, "ea"),
        P(None, None, "ea"),
        P(None, "ea", None),
        P(None, "ea", None),
        P(None, "ea", None),
        P(None, "ea", None, row),
        P(None, "ea", row, None),
    )
    return jax.shard_map(
        per_device, mesh=fine, in_specs=in_specs, out_specs=out_specs, check_vma=False
    )
```

```python
import jax
import jax.numpy as jnp
from jax import lax
from jax.experimental import pallas as pl
from jax.experimental.pallas import tpu as pltpu
from jax.sharding import Mesh
from jax.sharding import PartitionSpec as P

HEADS = 12
HEAD = 64
SEQ = 197
LAYERS = 2
EPS = 1e-06
HIGH = lax.Precision.HIGHEST
BF = jnp.bfloat16
F32 = jnp.float32
SLOTS = 16
SCALE = HEAD ** (-0.5)
GROUP = ("ea", "half")


def dot(a, b, dims=((1,), (0,))):
    return lax.dot_general(a, b, (dims, ((), ())), preferred_element_type=F32)


def dot_nt(a, b):
    return dot(a, b, ((1,), (1,)))


def dot_tn(a, b):
    return dot(a, b, ((0,), (0,)))


def swap_core(value):
    return lax.ppermute(value, "core", [(0, 1), (1, 0)])


def swap_half(value):
    return lax.ppermute(value, "half", [(0, 1), (1, 0)])


def exchange(rows):
    return lax.all_to_all(rows, GROUP, split_axis=0, concat_axis=0, tiled=True)


def gelu_parts(x):
    mag = jnp.abs(x)
    t = 1.0 / (1.0 + (0.3275911 * 0.7071067811865476) * mag)
    bell = jnp.exp(-0.5 * x * x)
    poly = 0.5 * t * (
        0.254829592
        + t * (-0.284496736 + t * (1.421413741 + t * (-1.453152027 + t * 1.061405429)))
    )
    tail = poly * bell
    cdf = jnp.where(x < 0, tail, 1.0 - tail)
    return cdf, cdf + x * bell * 0.3989422804014327


def normalize(x, gain, bias):
    center = jnp.mean(x, axis=-1, keepdims=True)
    shifted = x - center
    spread = jnp.mean(shifted * shifted, axis=-1, keepdims=True)
    inv = lax.rsqrt(spread + EPS)
    unit = shifted * inv
    return unit * gain + bias, unit, inv


def normalize_back(grad, unit, inv, gain):
    scaled = grad * gain
    mean_a = jnp.mean(scaled, axis=-1, keepdims=True)
    mean_b = jnp.mean(scaled * unit, axis=-1, keepdims=True)
    return (
        inv * (scaled - mean_a - unit * mean_b),
        jnp.sum(grad * unit, axis=0),
        jnp.sum(grad, axis=0),
    )


def heads_of(matrix):
    return matrix.reshape(SEQ, HEADS, HEAD)


def gather_cols(mine, after=None):
    groups = lax.axis_size("ea")
    if after is not None:
        mine, _ = lax.optimization_barrier((mine, after))
    sent = jnp.broadcast_to(mine[None], (groups,) + mine.shape)
    got = lax.all_to_all(sent, "ea", split_axis=0, concat_axis=0)
    return got.reshape(-1, mine.shape[1])


def core_half(value, which=0):
    n = value.shape[1] // 2
    core = lax.axis_index("core")
    return lax.dynamic_slice_in_dim(value, (core if which == 0 else 1 - core) * n, n, 1)


def in_order(own, other):
    first = lax.axis_index("core") == 0
    return jnp.concatenate(
        [jnp.where(first, own, other), jnp.where(first, other, own)], axis=1
    )


def thirds(value):
    n = value.shape[1] // 3
    return [value[:, i * n : (i + 1) * n] for i in range(3)]


def core_dense(qkv, out, small):
    return jnp.concatenate([core_half(part) for part in thirds(qkv)] + [core_half(out), small], axis=1)


def split_dense(own, experts):
    other = swap_core(own[:, :1536])
    small = own[:, 1536:]
    norms = small[:, experts : experts + 4].astype(F32).T
    return (
        (own[:, :1152], other[:, :1152]),
        (own[:, 1152:1536], other[:, 1152:]),
        small,
        norms,
    )


def sum_send(grad_qkv, grad_out, small):
    give = [grad_qkv[1].astype(BF), grad_out[1].astype(BF), small.astype(BF)]
    own = [grad_qkv[0], grad_out[0], small]
    return jnp.concatenate(
        [(o + swap_core(g).astype(F32)).astype(BF) for o, g in zip(own, give)], axis=1
    )


def sum_exchange(pair, after=None):
    groups = lax.axis_size("ea")
    if after is not None:
        pair, _ = lax.optimization_barrier((pair, after))
    return lax.all_to_all(
        pair.reshape(groups, -1, pair.shape[1]), "ea", split_axis=0, concat_axis=0
    )


def sum_finish(parts):
    part = jnp.sum(parts.astype(F32), axis=0)
    full = part + swap_half(part)
    other = swap_core(full[:, :1536])
    qkv = [
        in_order(own, more) for own, more in zip(thirds(full[:, :1152]), thirds(other[:, :1152]))
    ]
    return (
        jnp.concatenate(qkv, axis=1),
        in_order(full[:, 1152:1536], other[:, 1152:]),
        full[:, 1536:],
    )


def pad_cols(value, cols):
    return jnp.pad(value, ((0, 0), (0, cols - value.shape[1])))


def softmax_rows(scores):
    expo = jnp.exp(scores - jnp.max(scores, axis=-1, keepdims=True))
    return expo * (1.0 / jnp.sum(expo, axis=-1, keepdims=True))


def place(core, side, start, size):
    half = core if side == 0 else 1 - core
    return pl.ds(pl.multiple_of(half * 384 + start, 128), size)


def masked(pair, j):
    lane = lax.broadcasted_iota(jnp.int32, pair.shape, 1)
    return jnp.where((lane < HEAD) == (j == 0), pair, jnp.zeros_like(pair))


def merge(first, second):
    lane = lax.broadcasted_iota(jnp.int32, first.shape, 1)
    return jnp.where(lane < HEAD, first, second)


def attend_kernel(
    core_ref, state, norms, qkv_o, qkv_x, out_o, out_x, small, normed, proj_o, proj_x, mixed, after,
    normed_two, logits,
):
    core = core_ref[0]
    wide, _, _ = normalize(state[...], norms[0:1, :], norms[2:3, :])
    normed[...] = wide.astype(BF)
    for side, weight, proj in ((0, qkv_o, proj_o), (1, qkv_x, proj_x)):
        proj[...] = dot(normed[...], weight[...]).astype(BF)
        for at in range(0, 384, 128):
            query, key_part, value_part = (proj[:, i * 384 + at : i * 384 + at + 128] for i in range(3))
            found = []
            for j in range(2):
                shares = softmax_rows(dot_nt(masked(query, j), key_part) * SCALE)
                found.append(dot(shares.astype(BF), value_part))
            mixed[:, place(core, side, at, 128)] = merge(*found).astype(BF)
    for side, weight in ((0, out_o), (1, out_x)):
        cols = place(core, side, 0, 384)
        after[:, cols] = state[:, cols] + dot(mixed[...], weight[...])
    wide, _, _ = normalize(after[...], norms[1:2, :], norms[3:4, :])
    normed_two[...] = wide.astype(BF)
    logits[...] = dot(normed_two[...], small[...])


def attend_back_kernel(
    core_ref, grad, grad_two, state, after, norms, proj_o, proj_x, qkv_o, qkv_x, out_o, out_x,
    grad_in, grad_attn, gp_o, gp_x, stats, grad_mixed,
):
    core = core_ref[0]
    _, unit, inv = normalize(after[...], norms[1:2, :], norms[3:4, :])
    part, gain_two, bias_two = normalize_back(grad_two[...], unit, inv, norms[1:2, :])
    grad_in[...] = grad[...] + part
    grad_attn[...] = grad_in[...].astype(BF)
    grad_mixed[...] = sum(
        dot_nt(grad_attn[:, place(core, side, 0, 384)], weight[...])
        for side, weight in ((0, out_o), (1, out_x))
    ).astype(BF)
    for side, proj, gp in ((0, proj_o, gp_o), (1, proj_x, gp_x)):
        for at in range(0, 384, 128):
            query, key_part, value_part = (proj[:, i * 384 + at : i * 384 + at + 128] for i in range(3))
            outer = grad_mixed[:, place(core, side, at, 128)]
            found = []
            for j in range(2):
                shares = softmax_rows(dot_nt(masked(query, j), key_part) * SCALE)
                grad_shares = dot_nt(masked(outer, j), value_part)
                inner = jnp.sum(grad_shares * shares, axis=-1, keepdims=True)
                raw = (shares * (grad_shares - inner) * SCALE).astype(BF)
                found.append(
                    (dot(raw, key_part), dot_tn(raw, query), dot_tn(shares.astype(BF), outer))
                )
            for i in range(3):
                gp[:, i * 384 + at : i * 384 + at + 128] = merge(found[0][i], found[1][i]).astype(BF)
    grad_normed = dot_nt(gp_o[...], qkv_o[...]) + dot_nt(gp_x[...], qkv_x[...])
    _, unit, inv = normalize(state[...], norms[0:1, :], norms[2:3, :])
    part, gain_one, bias_one = normalize_back(grad_normed, unit, inv, norms[0:1, :])
    grad_in[...] = grad_in[...] + part
    for i, row in enumerate((gain_one, gain_two, bias_one, bias_two)):
        stats[i : i + 1, :] = row[None, :]


def whole_call(kernel, args, outs, flops, scratch=()):
    core = lax.axis_index("core").astype(jnp.int32).reshape(1)
    vmem = pl.BlockSpec(memory_space=pltpu.VMEM)
    return pl.pallas_call(
        kernel,
        in_specs=[pl.BlockSpec(memory_space=pltpu.SMEM)] + [vmem] * len(args),
        out_specs=[vmem] * len(outs),
        out_shape=[jax.ShapeDtypeStruct(shape, kind) for shape, kind in outs],
        scratch_shapes=list(scratch),
        compiler_params=pltpu.CompilerParams(vmem_limit_bytes=48 * 1024 * 1024),
        cost_estimate=pl.CostEstimate(flops=flops, bytes_accessed=8 << 20, transcendentals=0),
    )(core, *args)


def attention(state, dense):
    qkv_w, out_w, small, norms = dense
    tokens, width = state.shape
    rows = lambda n, kind: ((tokens, n), kind)
    normed, proj_o, proj_x, mixed, after, normed_two, logits = whole_call(
        attend_kernel,
        [state, norms, *qkv_w, *out_w, small],
        [
            rows(width, BF), rows(1152, BF), rows(1152, BF), rows(width, BF), rows(width, F32),
            rows(width, BF), rows(128, F32),
        ],
        4 * tokens * width * (4 * width + 4 * tokens),
    )
    return after, normed_two, logits, (state, normed, proj_o, proj_x, mixed, after)


def attention_back(grad, grad_two, kept, dense):
    state, normed, proj_o, proj_x, mixed, after = kept
    qkv_w, out_w, _, norms = dense
    tokens, width = grad.shape
    rows = lambda n, kind: ((tokens, n), kind)
    grad_in, grad_attn, gp_o, gp_x, stats = whole_call(
        attend_back_kernel,
        [grad, grad_two, state, after, norms, proj_o, proj_x, *qkv_w, *out_w],
        [rows(width, F32), rows(width, BF), rows(1152, BF), rows(1152, BF), ((4, width), F32)],
        8 * tokens * width * (4 * width + 8 * tokens),
        [pltpu.VMEM((tokens, width), BF)],
    )
    return grad_in, stats, (normed, gp_o, gp_x, mixed, grad_attn)


def dense_grads(normed, gp_o, gp_x, mixed, grad_attn):
    grad_out = [dot_tn(mixed, core_half(grad_attn, which)) for which in (0, 1)]
    return [dot_tn(normed, gp_o), dot_tn(normed, gp_x)], grad_out


def forward_kernel(rows, w_in, w_out, hidden, slope, part):
    pre = dot(rows[...], w_in[...])
    cdf, steep = gelu_parts(pre)
    hidden[...] = (pre * cdf).astype(BF)
    slope[...] = steep.astype(BF)
    part[...] = dot(hidden[...], w_out[...]).astype(BF)


def backward_kernel(grows, slope, w_in, w_out, grad_pre, part):
    grad_hidden = dot_nt(grows[...], w_out[...])
    grad_pre[...] = (grad_hidden * slope[...].astype(F32)).astype(BF)
    part[...] = dot_nt(grad_pre[...], w_in[...]).astype(BF)


def both_kernel(rows, w_in, w_out, hidden, grad_pre, part):
    width = w_in.shape[0]
    pre = dot(rows[:, :width], w_in[...])
    cdf, steep = gelu_parts(pre)
    hidden[...] = (pre * cdf).astype(BF)
    part[:, :width] = dot(hidden[...], w_out[...]).astype(BF)
    grad_hidden = dot_nt(rows[:, width:], w_out[...])
    grad_pre[...] = (grad_hidden * steep).astype(BF)
    part[:, width:] = dot_nt(grad_pre[...], w_in[...]).astype(BF)


BLOCK = 512


def expert_call(kernel, row_args, weights, out_widths, products):
    count = row_args[0].shape[0]

    def rows_spec(width):
        return pl.BlockSpec((BLOCK, width), lambda i: (i, 0))

    moved = sum(a.size for a in row_args) + sum(w.size for w in weights) + count * sum(out_widths)
    return pl.pallas_call(
        kernel,
        grid=(count // BLOCK,),
        in_specs=[rows_spec(a.shape[1]) for a in row_args]
        + [pl.BlockSpec(w.shape, lambda i: (0, 0)) for w in weights],
        out_specs=[rows_spec(width) for width in out_widths],
        out_shape=[jax.ShapeDtypeStruct((count, width), BF) for width in out_widths],
        compiler_params=pltpu.CompilerParams(vmem_limit_bytes=48 * 1024 * 1024),
        cost_estimate=pl.CostEstimate(
            flops=2 * count * 768 * 768 * products, bytes_accessed=2 * moved, transcendentals=0
        ),
    )(*row_args, *weights)


def join_cores(part_own, part_other):
    return (part_own.astype(F32) + swap_core(part_other).astype(F32)).astype(BF)


def routing(chosen, experts):
    tokens = chosen.shape[0]
    flat = jnp.concatenate([chosen[:, 0], chosen[:, 1]])
    onehot = flat[:, None] == jnp.arange(experts, dtype=jnp.int32)[None, :]
    pairs = 2 * tokens
    earlier = (
        lax.broadcasted_iota(jnp.int32, (pairs, pairs), 1)
        < lax.broadcasted_iota(jnp.int32, (pairs, pairs), 0)
    ).astype(BF)
    onehot = onehot.astype(F32)
    before = dot(earlier, onehot.astype(BF))
    position = jnp.sum(before * onehot, axis=1).astype(jnp.int32)
    code = flat * (2 * SLOTS) + position
    slots = experts * 2 * SLOTS
    row_code = lax.broadcasted_iota(jnp.int32, (slots, pairs), 0)
    row_code = row_code - jnp.where(lax.rem(row_code, 2 * SLOTS) >= SLOTS, SLOTS, 0)
    send = (row_code == code[None, :]).astype(BF)
    col_code = lax.broadcasted_iota(jnp.int32, (pairs, slots), 1)
    col_code = col_code - jnp.where(lax.rem(col_code, 2 * SLOTS) >= SLOTS, SLOTS, 0)
    fetch = (col_code == code[:, None]).astype(BF)
    return onehot, send, fetch


def router_forward(logits, onehot):
    router = jax.nn.softmax(logits, axis=-1)
    tokens = router.shape[0]
    gate = [
        jnp.sum(onehot[j * tokens : (j + 1) * tokens] * router, axis=1, keepdims=True)
        for j in range(2)
    ]
    return router, gate


def router_back(grad, picked, router, onehot, normed_two, router_w):
    tokens = router.shape[0]
    grad_router = 0.0
    for j in range(2):
        part = jnp.sum(grad * picked[j], axis=1, keepdims=True)
        grad_router = grad_router + onehot[j * tokens : (j + 1) * tokens] * part
    grad_logit = router * (grad_router - jnp.sum(grad_router * router, axis=-1, keepdims=True))
    grad_normed = jnp.dot(grad_logit, router_w.astype(F32).T, precision=HIGH)
    grad_router_w = jnp.dot(normed_two.astype(F32).T, grad_logit, precision=HIGH)
    return grad_normed, grad_router_w


def small_grads(grad_router_w, stats):
    return pad_cols(jnp.concatenate([grad_router_w, stats.T], axis=1), 128)


def per_device(
    image_tokens,
    cotangent,
    routes,
    norm_gains,
    norm_biases,
    qkv_weight,
    out_weight,
    router_weight,
    expert_in,
    expert_out,
):
    tokens, width = image_tokens.shape
    experts = lax.axis_size("ea")
    mine = []
    for b in range(LAYERS):
        small = jnp.concatenate([router_weight[b], norm_gains[b].T, norm_biases[b].T], axis=1)
        mine.append(core_dense(qkv_weight[b], out_weight[b], pad_cols(small, 128)))
    dense0 = split_dense(gather_cols(mine[0]), experts)
    routed = [routing(routes[b], experts) for b in range(LAYERS)]
    w_in = [expert_in[b, 0] for b in range(LAYERS)]
    w_out = [expert_out[b, 0] for b in range(LAYERS)]

    state = image_tokens.astype(F32)
    after0, normed0, logits, kept0 = attention(state, dense0)
    onehot, send, fetch = routed[0]
    router0, gate0 = router_forward(logits[:, :experts], onehot)
    arrived = exchange(dot(send[:, :tokens] + send[:, tokens:], normed0).astype(BF))
    gathered1 = gather_cols(mine[1], after=arrived)
    rows0 = (arrived, swap_core(arrived))
    first = [
        expert_call(forward_kernel, [r], [w_in[0], w_out[0]], [width] * 3, 2) for r in rows0
    ]
    hidden0, slope0, part = zip(*first)
    returned = exchange(join_cores(*part))
    dense1 = split_dense(gathered1, experts)
    picked = dot(fetch, returned)
    picked0 = (picked[:tokens], picked[tokens:])
    state1 = after0 + gate0[0] * picked0[0] + gate0[1] * picked0[1]

    grad = cotangent.astype(F32)
    after1, normed1, logits, kept1 = attention(state1, dense1)
    onehot1, send1, fetch1 = routed[1]
    router1, gate1 = router_forward(logits[:, :experts], onehot1)
    rows = dot(send1[:, :tokens] + send1[:, tokens:], normed1).astype(BF)
    grad_rows = jnp.concatenate([(g * grad).astype(BF) for g in gate1], axis=0)
    grad_rows = dot(send1, grad_rows).astype(BF)
    arrived = exchange(jnp.concatenate([rows, grad_rows], axis=1))
    both = (arrived, swap_core(arrived))
    second = [
        expert_call(both_kernel, [r], [w_in[1], w_out[1]], [width, width, 2 * width], 4)
        for r in both
    ]
    hidden1, grad_pre1, part = zip(*second)
    returned = exchange(join_cores(*part))
    picked = dot(fetch1, returned)
    picked1 = (picked[:tokens, :width], picked[tokens:, :width])
    grad_sent = picked[:tokens, width:] + picked[tokens:, width:]
    block_out = (after1 + gate1[0] * picked1[0] + gate1[1] * picked1[1]).astype(BF)
    grad_w_out1 = sum(dot_tn(h, r[:, width:]) for h, r in zip(hidden1, both))
    grad_w_in1 = sum(dot_tn(r[:, :width], g) for r, g in zip(both, grad_pre1))

    extra, grad_router_w1 = router_back(
        grad, picked1, router1, onehot1, normed1, dense1[2][:, :experts]
    )
    grad, stats1, terms1 = attention_back(grad, grad_sent + extra, kept1, dense1)

    grad_rows = jnp.concatenate([(g * grad).astype(BF) for g in gate0], axis=0)
    arrived = exchange(dot(send, grad_rows).astype(BF))
    grows0 = (arrived, swap_core(arrived))
    third = [
        expert_call(backward_kernel, [r, s], [w_in[0], w_out[0]], [width] * 2, 2)
        for r, s in zip(grows0, slope0)
    ]
    grad_pre0, part = zip(*third)
    pair1 = sum_send(*dense_grads(*terms1), small_grads(grad_router_w1, stats1))
    returned = exchange(join_cores(*part))
    parts1 = sum_exchange(pair1, after=returned)
    picked = dot(fetch, returned)
    grad_sent = picked[:tokens] + picked[tokens:]
    grad_w_out0 = sum(dot_tn(h, g) for h, g in zip(hidden0, grows0))
    grad_w_in0 = sum(dot_tn(r, g) for r, g in zip(rows0, grad_pre0))
    extra, grad_router_w0 = router_back(
        grad, picked0, router0, onehot, normed0, dense0[2][:, :experts]
    )
    grad, stats0, terms0 = attention_back(grad, grad_sent + extra, kept0, dense0)
    terms0, parts1 = lax.optimization_barrier((terms0, parts1))
    pair0 = sum_send(*dense_grads(*terms0), small_grads(grad_router_w0, stats0))
    parts0 = sum_exchange(pair0)
    sums1 = sum_finish(parts1)
    sums0 = sum_finish(parts0)

    qkv_sum, out_sum, small = (jnp.stack(pair) for pair in zip(sums0, sums1))
    return (
        block_out,
        grad,
        small[:, :, experts : experts + 2].transpose(0, 2, 1),
        small[:, :, experts + 2 : experts + 4].transpose(0, 2, 1),
        qkv_sum,
        out_sum,
        small[:, :, :experts],
        jnp.stack([grad_w_in0, grad_w_in1])[:, None],
        jnp.stack([grad_w_out0, grad_w_out1])[:, None],
    )


def solution(mesh):
    fine = Mesh(
        mesh.devices.reshape(mesh.shape["ea"], mesh.shape["row"] // 2, 2), ("ea", "half", "core")
    )
    row = ("half", "core")
    every = ("ea",) + row
    in_specs = (
        P(every, None),
        P(every, None),
        P(None, every, None),
        P(None, None, "ea"),
        P(None, None, "ea"),
        P(None, "ea", None),
        P(None, "ea", None),
        P(None, "ea", None),
        P(None, "ea", None, row),
        P(None, "ea", row, None),
    )
    out_specs = (
        P(every, None),
        P(every, None),
        P(None, None, "ea"),
        P(None, None, "ea"),
        P(None, "ea", None),
        P(None, "ea", None),
        P(None, "ea", None),
        P(None, "ea", None, row),
        P(None, "ea", row, None),
    )
    return jax.shard_map(
        per_device, mesh=fine, in_specs=in_specs, out_specs=out_specs, check_vma=False
    )
```

```python
import functools

import jax
import jax.numpy as jnp
from jax import lax
from jax.experimental import pallas as pl
from jax.experimental.pallas import tpu as pltpu
from jax.sharding import Mesh
from jax.sharding import PartitionSpec as P

HEADS = 12
HEAD = 64
SEQ = 197
LAYERS = 2
EPS = 1e-06
HIGH = lax.Precision.HIGHEST
BF = jnp.bfloat16
F32 = jnp.float32
SLOTS = 16
SCALE = HEAD ** (-0.5)
GROUP = ("ea", "half")
VMEM = 28 * 1024 * 1024


def dot(a, b, dims=((1,), (0,))):
    return lax.dot_general(a, b, (dims, ((), ())), preferred_element_type=F32)


def dot_nt(a, b):
    return dot(a, b, ((1,), (1,)))


def dot_tn(a, b):
    return dot(a, b, ((0,), (0,)))


def swap_core(value):
    return lax.ppermute(value, "core", [(0, 1), (1, 0)])


def exchange(rows):
    return lax.all_to_all(rows, GROUP, split_axis=0, concat_axis=0, tiled=True)


def gelu_parts(x):
    base = 1.0 + (0.3275911 * 0.7071067811865476) * jnp.abs(x)
    t = pl.reciprocal(base, approx=True)
    t = t * (2.0 - base * t)
    bell = jnp.exp2((x * x) * (-0.5 * 1.4426950408889634))
    poly = t * (
        0.5 * 0.254829592
        + t
        * (
            0.5 * -0.284496736
            + t * (0.5 * 1.421413741 + t * (0.5 * -1.453152027 + t * (0.5 * 1.061405429)))
        )
    )
    tail = poly * bell
    cdf = jnp.where(x < 0, tail, 1.0 - tail)
    return cdf, cdf + x * (bell * 0.3989422804014327)


def normalize(x, gain, bias):
    center = jnp.mean(x, axis=-1, keepdims=True)
    shifted = x - center
    spread = jnp.mean(shifted * shifted, axis=-1, keepdims=True)
    inv = lax.rsqrt(spread + EPS)
    unit = shifted * inv
    return unit * gain + bias, unit, inv


def normalize_back(grad, unit, inv, gain):
    scaled = grad * gain
    mean_a = jnp.mean(scaled, axis=-1, keepdims=True)
    mean_b = jnp.mean(scaled * unit, axis=-1, keepdims=True)
    return (
        inv * (scaled - mean_a - unit * mean_b),
        jnp.sum(grad * unit, axis=0),
        jnp.sum(grad, axis=0),
    )


def heads_of(matrix):
    return matrix.reshape(SEQ, HEADS, HEAD)


def gather_cols(mine, after=None):
    groups = lax.axis_size("ea")
    if after is not None:
        mine, _ = lax.optimization_barrier((mine, after))
    sent = jnp.broadcast_to(mine[None], (groups,) + mine.shape)
    got = lax.all_to_all(sent, "ea", split_axis=0, concat_axis=0)
    return got.reshape(-1, mine.shape[1])


def core_half(value, which=0):
    n = value.shape[1] // 2
    core = lax.axis_index("core")
    return lax.dynamic_slice_in_dim(value, (core if which == 0 else 1 - core) * n, n, 1)


def in_order(own, other):
    first = lax.axis_index("core") == 0
    return jnp.concatenate(
        [jnp.where(first, own, other), jnp.where(first, other, own)], axis=1
    )


def thirds(value):
    n = value.shape[1] // 3
    return [value[:, i * n : (i + 1) * n] for i in range(3)]


def core_dense(qkv, out, small):
    return jnp.concatenate([core_half(part) for part in thirds(qkv)] + [core_half(out), small], axis=1)


def split_dense(own):
    return own, swap_core(own)


def sum_send(grad_qkv, grad_out, small):
    give = [grad_qkv[1].astype(BF), grad_out[1].astype(BF), small.astype(BF)]
    own = [grad_qkv[0], grad_out[0], small]
    return jnp.concatenate(
        [(o + swap_core(g).astype(F32)).astype(BF) for o, g in zip(own, give)], axis=1
    )


def sum_exchange(pair, after=None):
    groups = lax.axis_size("ea")
    if after is not None:
        pair, _ = lax.optimization_barrier((pair, after))
    return lax.all_to_all(
        pair.reshape(groups, -1, pair.shape[1]), "ea", split_axis=0, concat_axis=0
    )


def swap_row(value, flip):
    return lax.ppermute(value, ("half", "core"), [(i, i ^ flip) for i in range(4)])


def sum_finish(parts):
    part = jnp.sum(parts.astype(F32), axis=0)
    full = part + swap_row(part, 2)
    dense = part[:, :1536]
    other = swap_row(dense, 1) + swap_row(dense, 3)
    qkv = [
        in_order(own, more) for own, more in zip(thirds(full[:, :1152]), thirds(other[:, :1152]))
    ]
    return (
        jnp.concatenate(qkv, axis=1),
        in_order(full[:, 1152:1536], other[:, 1152:]),
        full[:, 1536:],
    )


def pad_cols(value, cols):
    return jnp.pad(value, ((0, 0), (0, cols - value.shape[1])))


def softmax_rows(scores):
    expo = jnp.exp(scores - jnp.max(scores, axis=-1, keepdims=True))
    return expo * (1.0 / jnp.sum(expo, axis=-1, keepdims=True))


def place(core, side, start, size):
    half = core if side == 0 else 1 - core
    return pl.ds(pl.multiple_of(half * 384 + start, 128), size)


def masked(pair, j):
    lane = lax.broadcasted_iota(jnp.int32, pair.shape, 1)
    return jnp.where((lane < HEAD) == (j == 0), pair, jnp.zeros_like(pair))


def merge(first, second):
    lane = lax.broadcasted_iota(jnp.int32, first.shape, 1)
    return jnp.where(lane < HEAD, first, second)


QKV = slice(0, 1152)
OUT = slice(1152, 1536)
SMALL = slice(1536, 1664)


def norms_of(own, experts):
    return own[:, SMALL].astype(F32).T[experts : experts + 4]


def attend_kernel(
    experts, core_ref, state, own, other, normed, proj_o, proj_x, mixed, after, normed_two, logits
):
    core = core_ref[0]
    norms = norms_of(own, experts)
    wide, _, _ = normalize(state[...], norms[0:1], norms[2:3])
    normed[...] = wide.astype(BF)
    for side, weight, proj in ((0, own, proj_o), (1, other, proj_x)):
        proj[...] = dot(normed[...], weight[:, QKV]).astype(BF)
        for at in range(0, 384, 128):
            query, key_part, value_part = (proj[:, i * 384 + at : i * 384 + at + 128] for i in range(3))
            found = []
            for j in range(2):
                shares = softmax_rows(dot_nt(masked(query, j), key_part) * SCALE)
                found.append(dot(shares.astype(BF), value_part))
            mixed[:, place(core, side, at, 128)] = merge(*found).astype(BF)
    for side, weight in ((0, own), (1, other)):
        cols = place(core, side, 0, 384)
        after[:, cols] = state[:, cols] + dot(mixed[...], weight[:, OUT])
    wide, _, _ = normalize(after[...], norms[1:2], norms[3:4])
    normed_two[...] = wide.astype(BF)
    logits[...] = dot(normed_two[...], own[:, SMALL])


def attend_back_kernel(
    experts, core_ref, grad, grad_two, state, after, proj_o, proj_x, own, other, grad_in, grad_attn,
    gp_o, gp_x, stats, grad_mixed,
):
    core = core_ref[0]
    norms = norms_of(own, experts)
    _, unit, inv = normalize(after[...], norms[1:2], norms[3:4])
    part, gain_two, bias_two = normalize_back(grad_two[...], unit, inv, norms[1:2])
    grad_in[...] = grad[...] + part
    grad_attn[...] = grad_in[...].astype(BF)
    grad_mixed[...] = sum(
        dot_nt(grad_attn[:, place(core, side, 0, 384)], weight[:, OUT])
        for side, weight in ((0, own), (1, other))
    ).astype(BF)
    for side, proj, gp in ((0, proj_o, gp_o), (1, proj_x, gp_x)):
        for at in range(0, 384, 128):
            query, key_part, value_part = (proj[:, i * 384 + at : i * 384 + at + 128] for i in range(3))
            outer = grad_mixed[:, place(core, side, at, 128)]
            found = []
            for j in range(2):
                shares = softmax_rows(dot_nt(masked(query, j), key_part) * SCALE)
                grad_shares = dot_nt(masked(outer, j), value_part)
                inner = jnp.sum(grad_shares * shares, axis=-1, keepdims=True)
                raw = (shares * (grad_shares - inner) * SCALE).astype(BF)
                found.append(
                    (dot(raw, key_part), dot_tn(raw, query), dot_tn(shares.astype(BF), outer))
                )
            for i in range(3):
                gp[:, i * 384 + at : i * 384 + at + 128] = merge(found[0][i], found[1][i]).astype(BF)
    grad_normed = dot_nt(gp_o[...], own[:, QKV]) + dot_nt(gp_x[...], other[:, QKV])
    _, unit, inv = normalize(state[...], norms[0:1], norms[2:3])
    part, gain_one, bias_one = normalize_back(grad_normed, unit, inv, norms[0:1])
    grad_in[...] = grad_in[...] + part
    for i, row in enumerate((gain_one, gain_two, bias_one, bias_two)):
        stats[i : i + 1, :] = row[None, :]


def whole_call(kernel, args, outs, flops, scratch=()):
    core = lax.axis_index("core").astype(jnp.int32).reshape(1)
    vmem = pl.BlockSpec(memory_space=pltpu.VMEM)
    return pl.pallas_call(
        kernel,
        in_specs=[pl.BlockSpec(memory_space=pltpu.SMEM)] + [vmem] * len(args),
        out_specs=[vmem] * len(outs),
        out_shape=[jax.ShapeDtypeStruct(shape, kind) for shape, kind in outs],
        scratch_shapes=list(scratch),
        compiler_params=pltpu.CompilerParams(vmem_limit_bytes=VMEM),
        cost_estimate=pl.CostEstimate(flops=flops, bytes_accessed=8 << 20, transcendentals=0),
    )(core, *args)


def attention(state, dense):
    tokens, width = state.shape
    rows = lambda n, kind: ((tokens, n), kind)
    normed, proj_o, proj_x, mixed, after, normed_two, logits = whole_call(
        functools.partial(attend_kernel, lax.axis_size("ea")),
        [state, *dense],
        [
            rows(width, BF), rows(1152, BF), rows(1152, BF), rows(width, BF), rows(width, F32),
            rows(width, BF), rows(128, F32),
        ],
        4 * tokens * width * (4 * width + 4 * tokens),
    )
    return after, normed_two, logits, (state, normed, proj_o, proj_x, mixed, after)


def attention_back(grad, grad_two, kept, dense):
    state, normed, proj_o, proj_x, mixed, after = kept
    tokens, width = grad.shape
    rows = lambda n, kind: ((tokens, n), kind)
    grad_in, grad_attn, gp_o, gp_x, stats = whole_call(
        functools.partial(attend_back_kernel, lax.axis_size("ea")),
        [grad, grad_two, state, after, proj_o, proj_x, *dense],
        [rows(width, F32), rows(width, BF), rows(1152, BF), rows(1152, BF), ((4, width), F32)],
        8 * tokens * width * (4 * width + 8 * tokens),
        [pltpu.VMEM((tokens, width), BF)],
    )
    return grad_in, stats, (normed, gp_o, gp_x, mixed, grad_attn)


def dense_grads(normed, gp_o, gp_x, mixed, grad_attn):
    grad_out = [dot_tn(mixed, core_half(grad_attn, which)) for which in (0, 1)]
    return [dot_tn(normed, gp_o), dot_tn(normed, gp_x)], grad_out


def forward_kernel(rows, w_in, w_out, hidden, slope, part):
    pre = dot(rows[...], w_in[0, 0])
    cdf, steep = gelu_parts(pre)
    hidden[...] = (pre * cdf).astype(BF)
    slope[...] = steep.astype(BF)
    part[...] = dot(hidden[...], w_out[0, 0]).astype(BF)


def backward_kernel(grows, slope, w_in, w_out, grad_pre, part):
    grad_hidden = dot_nt(grows[...], w_out[0, 0])
    grad_pre[...] = (grad_hidden * slope[...].astype(F32)).astype(BF)
    part[...] = dot_nt(grad_pre[...], w_in[0, 0]).astype(BF)


def both_kernel(rows, w_in, w_out, hidden, grad_pre, part):
    groups, _, slots, width = rows.shape
    pre = dot(rows[:, 0].reshape(groups * slots, width), w_in[0, 0])
    cdf, steep = gelu_parts(pre)
    hidden[...] = (pre * cdf).astype(BF)
    out = dot(hidden[...], w_out[0, 0]).astype(BF)
    part[:, 0] = out.reshape(groups, slots, width)
    grad_hidden = dot_nt(rows[:, 1].reshape(groups * slots, width), w_out[0, 0])
    grad_pre[...] = (grad_hidden * steep).astype(BF)
    out = dot_nt(grad_pre[...], w_in[0, 0]).astype(BF)
    part[:, 1] = out.reshape(groups, slots, width)


GROUPS = 32


def expert_call(kernel, depth, row_args, weights, out_dims, products):
    def spec(shape):
        block = (GROUPS * SLOTS,) + shape[1:] if len(shape) == 2 else (GROUPS,) + shape[1:]
        return pl.BlockSpec(block, lambda i: (i,) + (0,) * (len(shape) - 1))

    hidden_units, width = weights[1].shape[2:]
    count = row_args[-1].shape[0] * (1 if row_args[-1].ndim == 2 else SLOTS)
    moved = count * width * (len(row_args) + len(out_dims)) + 2 * hidden_units * width
    return pl.pallas_call(
        kernel,
        grid=(count // (GROUPS * SLOTS),),
        in_specs=[spec(a.shape) for a in row_args]
        + [pl.BlockSpec((1,) + w.shape[1:], lambda i: (depth, 0, 0, 0)) for w in weights],
        out_specs=[spec(shape) for shape in out_dims],
        out_shape=[jax.ShapeDtypeStruct(shape, BF) for shape in out_dims],
        compiler_params=pltpu.CompilerParams(vmem_limit_bytes=VMEM),
        cost_estimate=pl.CostEstimate(
            flops=2 * count * hidden_units * width * products,
            bytes_accessed=2 * moved,
            transcendentals=0,
        ),
    )(*row_args, *weights)


def join_cores(part_own, part_other):
    return (part_own.astype(F32) + swap_core(part_other).astype(F32)).astype(BF)


def routing(chosen, experts):
    flat = jnp.concatenate([chosen[:, 0], chosen[:, 1]])
    onehot = flat[:, None] == jnp.arange(experts, dtype=jnp.int32)[None, :]
    pairs = flat.shape[0]
    earlier = (
        lax.broadcasted_iota(jnp.int32, (pairs, pairs), 1)
        < lax.broadcasted_iota(jnp.int32, (pairs, pairs), 0)
    ).astype(BF)
    onehot = onehot.astype(F32)
    before = dot(earlier, onehot.astype(BF))
    position = jnp.sum(before * onehot, axis=1).astype(jnp.int32)
    return onehot, flat * SLOTS + position


def slot_codes(slots, kinds, dims, axis):
    row = lax.broadcasted_iota(jnp.int32, dims, axis)
    run = row // SLOTS
    return lax.rem(run, kinds), (run // (2 * kinds)) * SLOTS + lax.rem(row, SLOTS)


def one_hots(code, slots, kinds, kind):
    pairs = code.shape[0]
    found = []
    for dims, axis, codes in (((slots, pairs), 0, code[None, :]), ((pairs, slots), 1, code[:, None])):
        kind_of, slot_of = slot_codes(slots, kinds, dims, axis)
        found.append(((slot_of == codes) & (kind_of == kind)).astype(BF))
    return found


def router_forward(logits, onehot):
    router = jax.nn.softmax(logits, axis=-1)
    tokens = router.shape[0]
    gate = [
        jnp.sum(onehot[j * tokens : (j + 1) * tokens] * router, axis=1, keepdims=True)
        for j in range(2)
    ]
    return router, gate


def router_back(grad, picked, router, onehot, normed_two, router_w):
    tokens = router.shape[0]
    grad_router = 0.0
    for j in range(2):
        part = jnp.sum(grad * picked[j], axis=1, keepdims=True)
        grad_router = grad_router + onehot[j * tokens : (j + 1) * tokens] * part
    grad_logit = router * (grad_router - jnp.sum(grad_router * router, axis=-1, keepdims=True))
    grad_normed = jnp.dot(grad_logit, router_w.astype(F32).T, precision=HIGH)
    grad_router_w = jnp.dot(normed_two.astype(F32).T, grad_logit, precision=HIGH)
    return grad_normed, grad_router_w


def small_grads(grad_router_w, stats):
    return pad_cols(jnp.concatenate([grad_router_w, stats.T], axis=1), 128)


def per_device(
    image_tokens,
    cotangent,
    routes,
    norm_gains,
    norm_biases,
    qkv_weight,
    out_weight,
    router_weight,
    expert_in,
    expert_out,
):
    tokens, width = image_tokens.shape
    experts = lax.axis_size("ea")
    mine = []
    for b in range(LAYERS):
        small = jnp.concatenate([router_weight[b], norm_gains[b].T, norm_biases[b].T], axis=1)
        mine.append(core_dense(qkv_weight[b], out_weight[b], pad_cols(small, 128)))
    dense0 = split_dense(gather_cols(mine[0]))
    weights = [expert_in, expert_out]
    onehot0, code = routing(routes[0], experts)
    send, fetch = one_hots(code, experts * 2 * SLOTS, 1, 0)
    onehot1, code = routing(routes[1], experts)
    send_rows, fetch_rows = one_hots(code, experts * 4 * SLOTS, 2, 0)
    send_grads, fetch_grads = one_hots(code, experts * 4 * SLOTS, 2, 1)
    send_rows = send_rows[:, :tokens] + send_rows[:, tokens:]
    fetch_grads = fetch_grads[:tokens] + fetch_grads[tokens:]
    send1 = jnp.concatenate([send_rows, send_grads], axis=1)
    fetch1 = jnp.concatenate([fetch_rows, fetch_grads], axis=0)

    state = image_tokens.astype(F32)
    after0, normed0, logits, kept0 = attention(state, dense0)
    router0, gate0 = router_forward(logits[:, :experts], onehot0)
    arrived = exchange(dot(send[:, :tokens] + send[:, tokens:], normed0).astype(BF))
    gathered1 = gather_cols(mine[1], after=arrived)
    rows0 = (arrived, swap_core(arrived))
    first = [
        expert_call(forward_kernel, 0, [r], weights, [r.shape] * 3, 2) for r in rows0
    ]
    hidden0, slope0, part = zip(*first)
    returned = exchange(join_cores(*part))
    dense1 = split_dense(gathered1)
    picked = dot(fetch, returned)
    picked0 = (picked[:tokens], picked[tokens:])
    state1 = after0 + gate0[0] * picked0[0] + gate0[1] * picked0[1]

    grad = cotangent.astype(F32)
    after1, normed1, logits, kept1 = attention(state1, dense1)
    router1, gate1 = router_forward(logits[:, :experts], onehot1)
    rows = jnp.concatenate([normed1] + [(g * grad).astype(BF) for g in gate1], axis=0)
    arrived = exchange(dot(send1, rows).astype(BF)).reshape(-1, 2, SLOTS, width)
    both = (arrived, swap_core(arrived))
    flat = (arrived.shape[0] * SLOTS, width)
    second = [
        expert_call(both_kernel, 1, [r], weights, [flat, flat, r.shape], 4) for r in both
    ]
    hidden1, grad_pre1, part = zip(*second)
    returned = exchange(join_cores(*part).reshape(-1, width))
    grad_w_out1 = sum(dot_tn(h, r[:, 1].reshape(flat)) for h, r in zip(hidden1, both))
    grad_w_in1 = sum(dot_tn(r[:, 0].reshape(flat), g) for r, g in zip(both, grad_pre1))
    returned, grad_w_out1, grad_w_in1 = lax.optimization_barrier(
        (returned, grad_w_out1, grad_w_in1)
    )
    picked = dot(fetch1, returned)
    picked1 = (picked[:tokens], picked[tokens : 2 * tokens])
    grad_sent = picked[2 * tokens :]
    block_out = (after1 + gate1[0] * picked1[0] + gate1[1] * picked1[1]).astype(BF)

    extra, grad_router_w1 = router_back(
        grad, picked1, router1, onehot1, normed1, dense1[0][:, 1536 : 1536 + experts]
    )
    grad, stats1, terms1 = attention_back(grad, grad_sent + extra, kept1, dense1)

    grad_rows = jnp.concatenate([(g * grad).astype(BF) for g in gate0], axis=0)
    arrived = exchange(dot(send, grad_rows).astype(BF))
    pair1 = sum_send(*dense_grads(*terms1), small_grads(grad_router_w1, stats1))
    arrived, pair1 = lax.optimization_barrier((arrived, pair1))
    grows0 = (arrived, swap_core(arrived))
    third = [
        expert_call(backward_kernel, 0, [r, s], weights, [r.shape] * 2, 2)
        for r, s in zip(grows0, slope0)
    ]
    grad_pre0, part = zip(*third)
    returned = exchange(join_cores(*part))
    parts1 = sum_exchange(pair1, after=returned)
    picked = dot(fetch, returned)
    grad_sent = picked[:tokens] + picked[tokens:]
    extra, grad_router_w0 = router_back(
        grad, picked0, router0, onehot0, normed0, dense0[0][:, 1536 : 1536 + experts]
    )
    grad, stats0, terms0 = attention_back(grad, grad_sent + extra, kept0, dense0)
    terms0, parts1 = lax.optimization_barrier((terms0, parts1))
    pair0 = sum_send(*dense_grads(*terms0), small_grads(grad_router_w0, stats0))
    parts0 = sum_exchange(pair0)
    (hidden0, grows0, rows0, grad_pre0), pair0 = lax.optimization_barrier(
        ((hidden0, grows0, rows0, grad_pre0), pair0)
    )
    grad_w_out0 = sum(dot_tn(h, g) for h, g in zip(hidden0, grows0))
    grad_w_in0 = sum(dot_tn(r, g) for r, g in zip(rows0, grad_pre0))
    sums1 = sum_finish(parts1)
    sums0 = sum_finish(parts0)

    qkv_sum, out_sum, small = (jnp.stack(pair) for pair in zip(sums0, sums1))
    return (
        block_out,
        grad,
        small[:, :, experts : experts + 2].transpose(0, 2, 1),
        small[:, :, experts + 2 : experts + 4].transpose(0, 2, 1),
        qkv_sum,
        out_sum,
        small[:, :, :experts],
        jnp.stack([grad_w_in0, grad_w_in1])[:, None],
        jnp.stack([grad_w_out0, grad_w_out1])[:, None],
    )


def solution(mesh):
    fine = Mesh(
        mesh.devices.reshape(mesh.shape["ea"], mesh.shape["row"] // 2, 2), ("ea", "half", "core")
    )
    row = ("half", "core")
    every = ("ea",) + row
    in_specs = (
        P(every, None),
        P(every, None),
        P(None, every, None),
        P(None, None, "ea"),
        P(None, None, "ea"),
        P(None, "ea", None),
        P(None, "ea", None),
        P(None, "ea", None),
        P(None, "ea", None, row),
        P(None, "ea", row, None),
    )
    out_specs = (
        P(every, None),
        P(every, None),
        P(None, None, "ea"),
        P(None, None, "ea"),
        P(None, "ea", None),
        P(None, "ea", None),
        P(None, "ea", None),
        P(None, "ea", None, row),
        P(None, "ea", row, None),
    )
    return jax.shard_map(
        per_device, mesh=fine, in_specs=in_specs, out_specs=out_specs, check_vma=False
    )
```

```python
import functools

import jax
import jax.numpy as jnp
from jax import lax
from jax.experimental import pallas as pl
from jax.experimental.pallas import tpu as pltpu
from jax.sharding import Mesh
from jax.sharding import PartitionSpec as P

HEADS = 12
HEAD = 64
SEQ = 197
LAYERS = 2
EPS = 1e-06
HIGH = lax.Precision.HIGHEST
BF = jnp.bfloat16
F32 = jnp.float32
SLOTS = 16
SCALE = HEAD ** (-0.5)
GROUP = ("ea", "half")
VMEM = 28 * 1024 * 1024


def dot(a, b, dims=((1,), (0,))):
    return lax.dot_general(a, b, (dims, ((), ())), preferred_element_type=F32)


def dot_nt(a, b):
    return dot(a, b, ((1,), (1,)))


def dot_tn(a, b):
    return dot(a, b, ((0,), (0,)))


def swap_core(value):
    return lax.ppermute(value, "core", [(0, 1), (1, 0)])


def exchange(rows):
    return lax.all_to_all(rows, GROUP, split_axis=0, concat_axis=0, tiled=True)


def gelu_parts(x):
    base = 1.0 + (0.3275911 * 0.7071067811865476) * jnp.abs(x)
    t = pl.reciprocal(base, approx=True)
    t = t * (2.0 - base * t)
    bell = jnp.exp2((x * x) * (-0.5 * 1.4426950408889634))
    poly = t * (
        0.5 * 0.254829592
        + t
        * (
            0.5 * -0.284496736
            + t * (0.5 * 1.421413741 + t * (0.5 * -1.453152027 + t * (0.5 * 1.061405429)))
        )
    )
    tail = poly * bell
    cdf = jnp.where(x < 0, tail, 1.0 - tail)
    return cdf, cdf + x * (bell * 0.3989422804014327)


def normalize(x, gain, bias):
    center = jnp.mean(x, axis=-1, keepdims=True)
    shifted = x - center
    spread = jnp.mean(shifted * shifted, axis=-1, keepdims=True)
    inv = lax.rsqrt(spread + EPS)
    unit = shifted * inv
    return unit * gain + bias, unit, inv


def normalize_back(grad, unit, inv, gain):
    scaled = grad * gain
    mean_a = jnp.mean(scaled, axis=-1, keepdims=True)
    mean_b = jnp.mean(scaled * unit, axis=-1, keepdims=True)
    return (
        inv * (scaled - mean_a - unit * mean_b),
        jnp.sum(grad * unit, axis=0),
        jnp.sum(grad, axis=0),
    )


def heads_of(matrix):
    return matrix.reshape(SEQ, HEADS, HEAD)


def gather_cols(mine, after=None):
    groups = lax.axis_size("ea")
    if after is not None:
        mine, _ = lax.optimization_barrier((mine, after))
    sent = jnp.broadcast_to(mine[None], (groups,) + mine.shape)
    got = lax.all_to_all(sent, "ea", split_axis=0, concat_axis=0)
    return got.reshape(-1, mine.shape[1])


def core_half(value, which=0):
    n = value.shape[1] // 2
    core = lax.axis_index("core")
    return lax.dynamic_slice_in_dim(value, (core if which == 0 else 1 - core) * n, n, 1)


def in_order(own, other):
    first = lax.axis_index("core") == 0
    return jnp.concatenate(
        [jnp.where(first, own, other), jnp.where(first, other, own)], axis=1
    )


def thirds(value):
    n = value.shape[1] // 3
    return [value[:, i * n : (i + 1) * n] for i in range(3)]


def core_dense(qkv, out, small):
    return jnp.concatenate([core_half(part) for part in thirds(qkv)] + [core_half(out), small], axis=1)


def split_dense(own):
    return own, swap_core(own)


def sum_send(own, give):
    return (own.astype(F32) + swap_core(give).astype(F32)).astype(BF)


def sum_exchange(pair, after=None):
    groups = lax.axis_size("ea")
    if after is not None:
        pair, _ = lax.optimization_barrier((pair, after))
    return lax.all_to_all(
        pair.reshape(groups, -1, pair.shape[1]), "ea", split_axis=0, concat_axis=0
    )


def swap_row(value, flip):
    return lax.ppermute(value, ("half", "core"), [(i, i ^ flip) for i in range(4)])


def sum_finish(parts):
    part = jnp.sum(parts.astype(F32), axis=0)
    full = part + swap_row(part, 2)
    dense = part[:, :1536]
    other = swap_row(dense, 1) + swap_row(dense, 3)
    qkv = [
        in_order(own, more) for own, more in zip(thirds(full[:, :1152]), thirds(other[:, :1152]))
    ]
    return (
        jnp.concatenate(qkv, axis=1),
        in_order(full[:, 1152:1536], other[:, 1152:]),
        full[:, 1536:],
    )


def pad_cols(value, cols):
    return jnp.pad(value, ((0, 0), (0, cols - value.shape[1])))


def softmax_rows(scores):
    expo = jnp.exp(scores - jnp.max(scores, axis=-1, keepdims=True))
    return expo * (1.0 / jnp.sum(expo, axis=-1, keepdims=True))


def place(core, side, start, size):
    half = core if side == 0 else 1 - core
    return pl.ds(pl.multiple_of(half * 384 + start, 128), size)


def masked(pair, j):
    lane = lax.broadcasted_iota(jnp.int32, pair.shape, 1)
    return jnp.where((lane < HEAD) == (j == 0), pair, jnp.zeros_like(pair))


def merge(first, second):
    lane = lax.broadcasted_iota(jnp.int32, first.shape, 1)
    return jnp.where(lane < HEAD, first, second)


QKV = slice(0, 1152)
OUT = slice(1152, 1536)
SMALL = slice(1536, 1664)


def norms_of(own, experts):
    return own[:, SMALL].astype(F32).T[experts : experts + 4]


def attend_kernel(
    experts, core_ref, state, own, other, normed, proj_o, proj_x, mixed, after, normed_two, logits
):
    core = core_ref[0]
    norms = norms_of(own, experts)
    wide, _, _ = normalize(state[...], norms[0:1], norms[2:3])
    normed[...] = wide.astype(BF)
    for side, weight, proj in ((0, own, proj_o), (1, other, proj_x)):
        proj[...] = dot(normed[...], weight[:, QKV]).astype(BF)
        for at in range(0, 384, 128):
            query, key_part, value_part = (proj[:, i * 384 + at : i * 384 + at + 128] for i in range(3))
            found = []
            for j in range(2):
                shares = softmax_rows(dot_nt(masked(query, j), key_part) * SCALE)
                found.append(dot(shares.astype(BF), value_part))
            mixed[:, place(core, side, at, 128)] = merge(*found).astype(BF)
    for side, weight in ((0, own), (1, other)):
        cols = place(core, side, 0, 384)
        after[:, cols] = state[:, cols] + dot(mixed[...], weight[:, OUT])
    wide, _, _ = normalize(after[...], norms[1:2], norms[3:4])
    normed_two[...] = wide.astype(BF)
    logits[...] = dot(normed_two[...], own[:, SMALL])


def attend_back_kernel(
    experts, core_ref, grad, grad_two, state, after, proj_o, proj_x, own, other, grad_in, grad_attn,
    gp_o, gp_x, stats, grad_mixed,
):
    core = core_ref[0]
    norms = norms_of(own, experts)
    _, unit, inv = normalize(after[...], norms[1:2], norms[3:4])
    part, gain_two, bias_two = normalize_back(grad_two[...], unit, inv, norms[1:2])
    grad_in[...] = grad[...] + part
    grad_attn[...] = grad_in[...].astype(BF)
    grad_mixed[...] = sum(
        dot_nt(grad_attn[:, place(core, side, 0, 384)], weight[:, OUT])
        for side, weight in ((0, own), (1, other))
    ).astype(BF)
    for side, proj, gp in ((0, proj_o, gp_o), (1, proj_x, gp_x)):
        for at in range(0, 384, 128):
            query, key_part, value_part = (proj[:, i * 384 + at : i * 384 + at + 128] for i in range(3))
            outer = grad_mixed[:, place(core, side, at, 128)]
            found = []
            for j in range(2):
                shares = softmax_rows(dot_nt(masked(query, j), key_part) * SCALE)
                grad_shares = dot_nt(masked(outer, j), value_part)
                inner = jnp.sum(grad_shares * shares, axis=-1, keepdims=True)
                raw = (shares * (grad_shares - inner) * SCALE).astype(BF)
                found.append(
                    (dot(raw, key_part), dot_tn(raw, query), dot_tn(shares.astype(BF), outer))
                )
            for i in range(3):
                gp[:, i * 384 + at : i * 384 + at + 128] = merge(found[0][i], found[1][i]).astype(BF)
    grad_normed = dot_nt(gp_o[...], own[:, QKV]) + dot_nt(gp_x[...], other[:, QKV])
    _, unit, inv = normalize(state[...], norms[0:1], norms[2:3])
    part, gain_one, bias_one = normalize_back(grad_normed, unit, inv, norms[0:1])
    grad_in[...] = grad_in[...] + part
    for i, row in enumerate((gain_one, gain_two, bias_one, bias_two)):
        stats[i : i + 1, :] = row[None, :]


def whole_call(kernel, args, outs, flops, scratch=()):
    core = lax.axis_index("core").astype(jnp.int32).reshape(1)
    vmem = pl.BlockSpec(memory_space=pltpu.VMEM)
    return pl.pallas_call(
        kernel,
        in_specs=[pl.BlockSpec(memory_space=pltpu.SMEM)] + [vmem] * len(args),
        out_specs=[vmem] * len(outs),
        out_shape=[jax.ShapeDtypeStruct(shape, kind) for shape, kind in outs],
        scratch_shapes=list(scratch),
        compiler_params=pltpu.CompilerParams(vmem_limit_bytes=VMEM),
        cost_estimate=pl.CostEstimate(flops=flops, bytes_accessed=1 << 16, transcendentals=0),
    )(core, *args)


def attention(state, dense):
    tokens, width = state.shape
    rows = lambda n, kind: ((tokens, n), kind)
    normed, proj_o, proj_x, mixed, after, normed_two, logits = whole_call(
        functools.partial(attend_kernel, lax.axis_size("ea")),
        [state, *dense],
        [
            rows(width, BF), rows(1152, BF), rows(1152, BF), rows(width, BF), rows(width, F32),
            rows(width, BF), rows(128, F32),
        ],
        1 << 20,
    )
    return after, normed_two, logits, (state, normed, proj_o, proj_x, mixed, after)


def attention_back(grad, grad_two, kept, dense):
    state, normed, proj_o, proj_x, mixed, after = kept
    tokens, width = grad.shape
    rows = lambda n, kind: ((tokens, n), kind)
    grad_in, grad_attn, gp_o, gp_x, stats = whole_call(
        functools.partial(attend_back_kernel, lax.axis_size("ea")),
        [grad, grad_two, state, after, proj_o, proj_x, *dense],
        [rows(width, F32), rows(width, BF), rows(1152, BF), rows(1152, BF), ((4, width), F32)],
        1 << 20,
        [pltpu.VMEM((tokens, width), BF)],
    )
    return grad_in, stats, (normed, gp_o, gp_x, mixed, grad_attn)


def dense_grad_kernel(core_ref, normed, gp_o, gp_x, mixed, grad_attn, small, own, give):
    core = core_ref[0]
    for side, gp, out in ((1, gp_x, give), (0, gp_o, own)):
        out[:, QKV] = dot_tn(normed[...], gp[...]).astype(BF)
        out[:, OUT] = dot_tn(mixed[...], grad_attn[:, place(core, side, 0, 384)]).astype(BF)
        out[:, SMALL] = small[...].astype(BF)


def dense_grads(normed, gp_o, gp_x, mixed, grad_attn, small):
    core = lax.axis_index("core").astype(jnp.int32).reshape(1)
    tokens, width = normed.shape
    rows = 256
    cols = pl.BlockSpec((tokens, rows), lambda i: (0, i))
    whole = pl.BlockSpec(memory_space=pltpu.VMEM)
    block = pl.BlockSpec((rows, 1664), lambda i: (i, 0))
    return pl.pallas_call(
        dense_grad_kernel,
        grid=(width // rows,),
        in_specs=[
            pl.BlockSpec(memory_space=pltpu.SMEM), cols, whole, whole, cols, whole,
            pl.BlockSpec((rows, 128), lambda i: (i, 0)),
        ],
        out_specs=[block, block],
        out_shape=[jax.ShapeDtypeStruct((width, 1664), BF)] * 2,
        compiler_params=pltpu.CompilerParams(vmem_limit_bytes=VMEM),
        cost_estimate=pl.CostEstimate(flops=1 << 20, bytes_accessed=1 << 16, transcendentals=0),
    )(core, normed, gp_o, gp_x, mixed, grad_attn, small)


def forward_kernel(rows, w_in, w_out, hidden, slope, part):
    pre = dot(rows[...], w_in[0, 0])
    cdf, steep = gelu_parts(pre)
    hidden[...] = (pre * cdf).astype(BF)
    slope[...] = steep.astype(BF)
    part[...] = dot(hidden[...], w_out[0, 0]).astype(BF)


def backward_kernel(grows, slope, w_in, w_out, grad_pre, part):
    grad_hidden = dot_nt(grows[...], w_out[0, 0])
    grad_pre[...] = (grad_hidden * slope[...].astype(F32)).astype(BF)
    part[...] = dot_nt(grad_pre[...], w_in[0, 0]).astype(BF)


def both_kernel(rows, w_in, w_out, hidden, grad_pre, part):
    groups, _, slots, width = rows.shape
    pre = dot(rows[:, 0].reshape(groups * slots, width), w_in[0, 0])
    cdf, steep = gelu_parts(pre)
    hidden[...] = (pre * cdf).astype(BF)
    out = dot(hidden[...], w_out[0, 0]).astype(BF)
    part[:, 0] = out.reshape(groups, slots, width)
    grad_hidden = dot_nt(rows[:, 1].reshape(groups * slots, width), w_out[0, 0])
    grad_pre[...] = (grad_hidden * steep).astype(BF)
    out = dot_nt(grad_pre[...], w_in[0, 0]).astype(BF)
    part[:, 1] = out.reshape(groups, slots, width)


GROUPS = 32


def expert_call(kernel, depth, row_args, weights, out_dims, products):
    def spec(shape):
        block = (GROUPS * SLOTS,) + shape[1:] if len(shape) == 2 else (GROUPS,) + shape[1:]
        return pl.BlockSpec(block, lambda i: (i,) + (0,) * (len(shape) - 1))

    hidden_units, width = weights[1].shape[2:]
    count = row_args[-1].shape[0] * (1 if row_args[-1].ndim == 2 else SLOTS)
    moved = count * width * (len(row_args) + len(out_dims)) + 2 * hidden_units * width
    return pl.pallas_call(
        kernel,
        grid=(count // (GROUPS * SLOTS),),
        in_specs=[spec(a.shape) for a in row_args]
        + [pl.BlockSpec((1,) + w.shape[1:], lambda i: (depth, 0, 0, 0)) for w in weights],
        out_specs=[spec(shape) for shape in out_dims],
        out_shape=[jax.ShapeDtypeStruct(shape, BF) for shape in out_dims],
        compiler_params=pltpu.CompilerParams(vmem_limit_bytes=VMEM),
        cost_estimate=pl.CostEstimate(
            flops=2 * count * hidden_units * width * products,
            bytes_accessed=2 * moved,
            transcendentals=0,
        ),
    )(*row_args, *weights)


def join_cores(part_own, part_other):
    return (part_own.astype(F32) + swap_core(part_other).astype(F32)).astype(BF)


def routing(chosen, experts):
    flat = jnp.concatenate([chosen[:, 0], chosen[:, 1]])
    onehot = flat[:, None] == jnp.arange(experts, dtype=jnp.int32)[None, :]
    pairs = flat.shape[0]
    earlier = (
        lax.broadcasted_iota(jnp.int32, (pairs, pairs), 1)
        < lax.broadcasted_iota(jnp.int32, (pairs, pairs), 0)
    ).astype(BF)
    onehot = onehot.astype(F32)
    before = dot(earlier, onehot.astype(BF))
    position = jnp.sum(before * onehot, axis=1).astype(jnp.int32)
    return onehot, flat * SLOTS + position


def slot_codes(slots, kinds, dims, axis):
    row = lax.broadcasted_iota(jnp.int32, dims, axis)
    run = row // SLOTS
    return lax.rem(run, kinds), (run // (2 * kinds)) * SLOTS + lax.rem(row, SLOTS)


def one_hots(code, slots, kinds, kind):
    pairs = code.shape[0]
    found = []
    for dims, axis, codes in (((slots, pairs), 0, code[None, :]), ((pairs, slots), 1, code[:, None])):
        kind_of, slot_of = slot_codes(slots, kinds, dims, axis)
        found.append(((slot_of == codes) & (kind_of == kind)).astype(BF))
    return found


def router_forward(logits, onehot):
    router = jax.nn.softmax(logits, axis=-1)
    tokens = router.shape[0]
    gate = [
        jnp.sum(onehot[j * tokens : (j + 1) * tokens] * router, axis=1, keepdims=True)
        for j in range(2)
    ]
    return router, gate


def router_back(grad, picked, router, onehot, normed_two, router_w):
    tokens = router.shape[0]
    grad_router = 0.0
    for j in range(2):
        part = jnp.sum(grad * picked[j], axis=1, keepdims=True)
        grad_router = grad_router + onehot[j * tokens : (j + 1) * tokens] * part
    grad_logit = router * (grad_router - jnp.sum(grad_router * router, axis=-1, keepdims=True))
    grad_normed = jnp.dot(grad_logit, router_w.astype(F32).T, precision=HIGH)
    grad_router_w = jnp.dot(normed_two.astype(F32).T, grad_logit, precision=HIGH)
    return grad_normed, grad_router_w


def small_grads(grad_router_w, stats):
    return pad_cols(jnp.concatenate([grad_router_w, stats.T], axis=1), 128)


def per_device(
    image_tokens,
    cotangent,
    routes,
    norm_gains,
    norm_biases,
    qkv_weight,
    out_weight,
    router_weight,
    expert_in,
    expert_out,
):
    tokens, width = image_tokens.shape
    experts = lax.axis_size("ea")
    mine = []
    for b in range(LAYERS):
        small = jnp.concatenate([router_weight[b], norm_gains[b].T, norm_biases[b].T], axis=1)
        mine.append(core_dense(qkv_weight[b], out_weight[b], pad_cols(small, 128)))
    dense0 = split_dense(gather_cols(mine[0]))
    weights = [expert_in, expert_out]
    onehot0, code = routing(routes[0], experts)
    send, fetch = one_hots(code, experts * 2 * SLOTS, 1, 0)
    onehot1, code = routing(routes[1], experts)
    send_rows, fetch_rows = one_hots(code, experts * 4 * SLOTS, 2, 0)
    send_grads, fetch_grads = one_hots(code, experts * 4 * SLOTS, 2, 1)
    send_rows = send_rows[:, :tokens] + send_rows[:, tokens:]
    fetch_grads = fetch_grads[:tokens] + fetch_grads[tokens:]
    send1 = jnp.concatenate([send_rows, send_grads], axis=1)
    fetch1 = jnp.concatenate([fetch_rows, fetch_grads], axis=0)

    state = image_tokens.astype(F32)
    after0, normed0, logits, kept0 = attention(state, dense0)
    router0, gate0 = router_forward(logits[:, :experts], onehot0)
    arrived = exchange(dot(send[:, :tokens] + send[:, tokens:], normed0).astype(BF))
    gathered1 = gather_cols(mine[1], after=arrived)
    rows0 = (arrived, swap_core(arrived))
    first = [
        expert_call(forward_kernel, 0, [r], weights, [r.shape] * 3, 2) for r in rows0
    ]
    hidden0, slope0, part = zip(*first)
    returned = exchange(join_cores(*part))
    dense1 = split_dense(gathered1)
    picked = dot(fetch, returned)
    picked0 = (picked[:tokens], picked[tokens:])
    state1 = after0 + gate0[0] * picked0[0] + gate0[1] * picked0[1]

    grad = cotangent.astype(F32)
    after1, normed1, logits, kept1 = attention(state1, dense1)
    router1, gate1 = router_forward(logits[:, :experts], onehot1)
    rows = jnp.concatenate([normed1] + [(g * grad).astype(BF) for g in gate1], axis=0)
    arrived = exchange(dot(send1, rows).astype(BF)).reshape(-1, 2, SLOTS, width)
    both = (arrived, swap_core(arrived))
    flat = (arrived.shape[0] * SLOTS, width)
    second = [
        expert_call(both_kernel, 1, [r], weights, [flat, flat, r.shape], 4) for r in both
    ]
    hidden1, grad_pre1, part = zip(*second)
    returned = exchange(join_cores(*part).reshape(-1, width))
    grad_w_out1 = sum(dot_tn(h, r[:, 1].reshape(flat)) for h, r in zip(hidden1, both))
    grad_w_in1 = sum(dot_tn(r[:, 0].reshape(flat), g) for r, g in zip(both, grad_pre1))
    returned, grad_w_out1, grad_w_in1 = lax.optimization_barrier(
        (returned, grad_w_out1, grad_w_in1)
    )
    picked = dot(fetch1, returned)
    picked1 = (picked[:tokens], picked[tokens : 2 * tokens])
    grad_sent = picked[2 * tokens :]
    block_out = (after1 + gate1[0] * picked1[0] + gate1[1] * picked1[1]).astype(BF)

    extra, grad_router_w1 = router_back(
        grad, picked1, router1, onehot1, normed1, dense1[0][:, 1536 : 1536 + experts]
    )
    grad, stats1, terms1 = attention_back(grad, grad_sent + extra, kept1, dense1)

    grad_rows = jnp.concatenate([(g * grad).astype(BF) for g in gate0], axis=0)
    arrived = exchange(dot(send, grad_rows).astype(BF))
    pair1 = sum_send(*dense_grads(*terms1, small_grads(grad_router_w1, stats1)))
    arrived, pair1 = lax.optimization_barrier((arrived, pair1))
    grows0 = (arrived, swap_core(arrived))
    third = [
        expert_call(backward_kernel, 0, [r, s], weights, [r.shape] * 2, 2)
        for r, s in zip(grows0, slope0)
    ]
    grad_pre0, part = zip(*third)
    returned = exchange(join_cores(*part))
    parts1 = sum_exchange(pair1, after=returned)
    picked = dot(fetch, returned)
    grad_sent = picked[:tokens] + picked[tokens:]
    extra, grad_router_w0 = router_back(
        grad, picked0, router0, onehot0, normed0, dense0[0][:, 1536 : 1536 + experts]
    )
    grad, stats0, terms0 = attention_back(grad, grad_sent + extra, kept0, dense0)
    pair0 = sum_send(*dense_grads(*terms0, small_grads(grad_router_w0, stats0)))
    pair0, parts1 = lax.optimization_barrier((pair0, parts1))
    parts0 = sum_exchange(pair0)
    (hidden0, grows0, rows0, grad_pre0), _ = lax.optimization_barrier(
        ((hidden0, grows0, rows0, grad_pre0), pair0)
    )
    grad_w_out0 = sum(dot_tn(h, g) for h, g in zip(hidden0, grows0))
    grad_w_in0 = sum(dot_tn(r, g) for r, g in zip(rows0, grad_pre0))
    (grad_w_out0, grad_w_in0), parts1 = lax.optimization_barrier(
        ((grad_w_out0, grad_w_in0), parts1)
    )
    sums1 = sum_finish(parts1)
    sums0 = sum_finish(parts0)

    qkv_sum, out_sum, small = (jnp.stack(pair) for pair in zip(sums0, sums1))
    return (
        block_out,
        grad,
        small[:, :, experts : experts + 2].transpose(0, 2, 1),
        small[:, :, experts + 2 : experts + 4].transpose(0, 2, 1),
        qkv_sum,
        out_sum,
        small[:, :, :experts],
        jnp.stack([grad_w_in0, grad_w_in1])[:, None],
        jnp.stack([grad_w_out0, grad_w_out1])[:, None],
    )


def solution(mesh):
    fine = Mesh(
        mesh.devices.reshape(mesh.shape["ea"], mesh.shape["row"] // 2, 2), ("ea", "half", "core")
    )
    row = ("half", "core")
    every = ("ea",) + row
    in_specs = (
        P(every, None),
        P(every, None),
        P(None, every, None),
        P(None, None, "ea"),
        P(None, None, "ea"),
        P(None, "ea", None),
        P(None, "ea", None),
        P(None, "ea", None),
        P(None, "ea", None, row),
        P(None, "ea", row, None),
    )
    out_specs = (
        P(every, None),
        P(every, None),
        P(None, None, "ea"),
        P(None, None, "ea"),
        P(None, "ea", None),
        P(None, "ea", None),
        P(None, "ea", None),
        P(None, "ea", None, row),
        P(None, "ea", row, None),
    )
    return jax.shard_map(
        per_device, mesh=fine, in_specs=in_specs, out_specs=out_specs, check_vma=False
    )
```

```python
import functools

import jax
import jax.numpy as jnp
from jax import lax
from jax.experimental import pallas as pl
from jax.experimental.pallas import tpu as pltpu
from jax.sharding import Mesh
from jax.sharding import PartitionSpec as P

HEADS = 12
HEAD = 64
SEQ = 197
LAYERS = 2
EPS = 1e-06
HIGH = lax.Precision.HIGHEST
BF = jnp.bfloat16
F32 = jnp.float32
SLOTS = 16
SCALE = HEAD ** (-0.5)
GROUP = ("ea", "half")
VMEM = 28 * 1024 * 1024


def dot(a, b, dims=((1,), (0,))):
    return lax.dot_general(a, b, (dims, ((), ())), preferred_element_type=F32)


def dot_nt(a, b):
    return dot(a, b, ((1,), (1,)))


def dot_tn(a, b):
    return dot(a, b, ((0,), (0,)))


def swap_core(value):
    return lax.ppermute(value, "core", [(0, 1), (1, 0)])


def exchange(rows):
    return lax.all_to_all(rows, GROUP, split_axis=0, concat_axis=0, tiled=True)


def gelu_parts(x):
    base = 1.0 + (0.3275911 * 0.7071067811865476) * jnp.abs(x)
    t = pl.reciprocal(base, approx=True)
    t = t * (2.0 - base * t)
    bell = jnp.exp2((x * x) * (-0.5 * 1.4426950408889634))
    poly = t * (
        0.5 * 0.254829592
        + t
        * (
            0.5 * -0.284496736
            + t * (0.5 * 1.421413741 + t * (0.5 * -1.453152027 + t * (0.5 * 1.061405429)))
        )
    )
    tail = poly * bell
    cdf = jnp.where(x < 0, tail, 1.0 - tail)
    return cdf, cdf + x * (bell * 0.3989422804014327)


def normalize(x, gain, bias):
    center = jnp.mean(x, axis=-1, keepdims=True)
    shifted = x - center
    spread = jnp.mean(shifted * shifted, axis=-1, keepdims=True)
    inv = lax.rsqrt(spread + EPS)
    unit = shifted * inv
    return unit * gain + bias, unit, inv


def normalize_back(grad, unit, inv, gain):
    scaled = grad * gain
    mean_a = jnp.mean(scaled, axis=-1, keepdims=True)
    mean_b = jnp.mean(scaled * unit, axis=-1, keepdims=True)
    return (
        inv * (scaled - mean_a - unit * mean_b),
        jnp.sum(grad * unit, axis=0),
        jnp.sum(grad, axis=0),
    )


def heads_of(matrix):
    return matrix.reshape(SEQ, HEADS, HEAD)


def gather_cols(mine, after=None):
    groups = lax.axis_size("ea")
    sent = jnp.broadcast_to(mine[None], (groups,) + mine.shape)
    if after is not None:
        sent, _ = lax.optimization_barrier((sent, after))
    got = lax.all_to_all(sent, "ea", split_axis=0, concat_axis=0)
    return got.reshape(-1, mine.shape[1])


def core_half(value, which=0):
    n = value.shape[1] // 2
    core = lax.axis_index("core")
    return lax.dynamic_slice_in_dim(value, (core if which == 0 else 1 - core) * n, n, 1)


def in_order(own, other):
    first = lax.axis_index("core") == 0
    return jnp.concatenate(
        [jnp.where(first, own, other), jnp.where(first, other, own)], axis=1
    )


def thirds(value):
    n = value.shape[1] // 3
    return [value[:, i * n : (i + 1) * n] for i in range(3)]


def core_dense(qkv, out, small):
    return jnp.concatenate([core_half(part) for part in thirds(qkv)] + [core_half(out), small], axis=1)


def split_dense(own):
    return own, swap_core(own)


def sum_send(own, give):
    return (own.astype(F32) + swap_core(give).astype(F32)).astype(BF)


def sum_exchange(pair):
    groups = lax.axis_size("ea")
    return lax.all_to_all(
        pair.reshape(groups, -1, pair.shape[1]), "ea", split_axis=0, concat_axis=0
    )


def swap_row(value, flip):
    return lax.ppermute(value, ("half", "core"), [(i, i ^ flip) for i in range(4)])


def sum_finish(parts):
    part = jnp.sum(parts.astype(F32), axis=0)
    full = part + swap_row(part, 2)
    dense = part[:, :1536]
    other = swap_row(dense, 1) + swap_row(dense, 3)
    qkv = [
        in_order(own, more) for own, more in zip(thirds(full[:, :1152]), thirds(other[:, :1152]))
    ]
    return (
        jnp.concatenate(qkv, axis=1),
        in_order(full[:, 1152:1536], other[:, 1152:]),
        full[:, 1536:],
    )


def pad_cols(value, cols):
    return jnp.pad(value, ((0, 0), (0, cols - value.shape[1])))


def softmax_rows(scores):
    expo = jnp.exp(scores - jnp.max(scores, axis=-1, keepdims=True))
    return expo * (1.0 / jnp.sum(expo, axis=-1, keepdims=True))


def place(core, side, start, size):
    half = core if side == 0 else 1 - core
    return pl.ds(pl.multiple_of(half * 384 + start, 128), size)


def masked(pair, j):
    lane = lax.broadcasted_iota(jnp.int32, pair.shape, 1)
    return jnp.where((lane < HEAD) == (j == 0), pair, jnp.zeros_like(pair))


def merge(first, second):
    lane = lax.broadcasted_iota(jnp.int32, first.shape, 1)
    return jnp.where(lane < HEAD, first, second)


QKV = slice(0, 1152)
OUT = slice(1152, 1536)
SMALL = slice(1536, 1664)


def norms_of(own, experts):
    return own[:, SMALL].astype(F32).T[experts : experts + 4]


def attend_kernel(
    experts, core_ref, state, own, other, normed, proj_o, proj_x, mixed, after, normed_two, logits
):
    core = core_ref[0]
    norms = norms_of(own, experts)
    wide, _, _ = normalize(state[...], norms[0:1], norms[2:3])
    normed[...] = wide.astype(BF)
    for side, weight, proj in ((0, own, proj_o), (1, other, proj_x)):
        proj[...] = dot(normed[...], weight[:, QKV]).astype(BF)
        for at in range(0, 384, 128):
            query, key_part, value_part = (proj[:, i * 384 + at : i * 384 + at + 128] for i in range(3))
            found = []
            for j in range(2):
                shares = softmax_rows(dot_nt(masked(query, j), key_part) * SCALE)
                found.append(dot(shares.astype(BF), value_part))
            mixed[:, place(core, side, at, 128)] = merge(*found).astype(BF)
    for side, weight in ((0, own), (1, other)):
        cols = place(core, side, 0, 384)
        after[:, cols] = state[:, cols] + dot(mixed[...], weight[:, OUT])
    wide, _, _ = normalize(after[...], norms[1:2], norms[3:4])
    normed_two[...] = wide.astype(BF)
    logits[...] = dot(normed_two[...], own[:, SMALL])


def attend_back_kernel(
    experts, core_ref, grad, grad_two, state, after, proj_o, proj_x, own, other, grad_in, grad_attn,
    gp_o, gp_x, stats, grad_mixed,
):
    core = core_ref[0]
    norms = norms_of(own, experts)
    _, unit, inv = normalize(after[...], norms[1:2], norms[3:4])
    part, gain_two, bias_two = normalize_back(grad_two[...], unit, inv, norms[1:2])
    grad_in[...] = grad[...] + part
    grad_attn[...] = grad_in[...].astype(BF)
    grad_mixed[...] = sum(
        dot_nt(grad_attn[:, place(core, side, 0, 384)], weight[:, OUT])
        for side, weight in ((0, own), (1, other))
    ).astype(BF)
    for side, proj, gp in ((0, proj_o, gp_o), (1, proj_x, gp_x)):
        for at in range(0, 384, 128):
            query, key_part, value_part = (proj[:, i * 384 + at : i * 384 + at + 128] for i in range(3))
            outer = grad_mixed[:, place(core, side, at, 128)]
            found = []
            for j in range(2):
                shares = softmax_rows(dot_nt(masked(query, j), key_part) * SCALE)
                grad_shares = dot_nt(masked(outer, j), value_part)
                inner = jnp.sum(grad_shares * shares, axis=-1, keepdims=True)
                raw = (shares * (grad_shares - inner) * SCALE).astype(BF)
                found.append(
                    (dot(raw, key_part), dot_tn(raw, query), dot_tn(shares.astype(BF), outer))
                )
            for i in range(3):
                gp[:, i * 384 + at : i * 384 + at + 128] = merge(found[0][i], found[1][i]).astype(BF)
    grad_normed = dot_nt(gp_o[...], own[:, QKV]) + dot_nt(gp_x[...], other[:, QKV])
    _, unit, inv = normalize(state[...], norms[0:1], norms[2:3])
    part, gain_one, bias_one = normalize_back(grad_normed, unit, inv, norms[0:1])
    grad_in[...] = grad_in[...] + part
    for i, row in enumerate((gain_one, gain_two, bias_one, bias_two)):
        stats[i : i + 1, :] = row[None, :]


def whole_call(kernel, args, outs, flops, scratch=()):
    core = lax.axis_index("core").astype(jnp.int32).reshape(1)
    vmem = pl.BlockSpec(memory_space=pltpu.VMEM)
    return pl.pallas_call(
        kernel,
        in_specs=[pl.BlockSpec(memory_space=pltpu.SMEM)] + [vmem] * len(args),
        out_specs=[vmem] * len(outs),
        out_shape=[jax.ShapeDtypeStruct(shape, kind) for shape, kind in outs],
        scratch_shapes=list(scratch),
        compiler_params=pltpu.CompilerParams(vmem_limit_bytes=VMEM),
        cost_estimate=pl.CostEstimate(flops=flops, bytes_accessed=8 << 20, transcendentals=0),
    )(core, *args)


def attention(state, dense):
    tokens, width = state.shape
    rows = lambda n, kind: ((tokens, n), kind)
    normed, proj_o, proj_x, mixed, after, normed_two, logits = whole_call(
        functools.partial(attend_kernel, lax.axis_size("ea")),
        [state, *dense],
        [
            rows(width, BF), rows(1152, BF), rows(1152, BF), rows(width, BF), rows(width, F32),
            rows(width, BF), rows(128, F32),
        ],
        4 * tokens * width * (4 * width + 4 * tokens),
    )
    return after, normed_two, logits, (state, normed, proj_o, proj_x, mixed, after)


def attention_back(grad, grad_two, kept, dense):
    state, normed, proj_o, proj_x, mixed, after = kept
    tokens, width = grad.shape
    rows = lambda n, kind: ((tokens, n), kind)
    grad_in, grad_attn, gp_o, gp_x, stats = whole_call(
        functools.partial(attend_back_kernel, lax.axis_size("ea")),
        [grad, grad_two, state, after, proj_o, proj_x, *dense],
        [rows(width, F32), rows(width, BF), rows(1152, BF), rows(1152, BF), ((4, width), F32)],
        8 * tokens * width * (4 * width + 8 * tokens),
        [pltpu.VMEM((tokens, width), BF)],
    )
    return grad_in, stats, (normed, gp_o, gp_x, mixed, grad_attn)


def dense_grad_kernel(core_ref, normed, gp_o, gp_x, mixed, grad_attn, small, own, give):
    core = core_ref[0]
    for side, gp, out in ((1, gp_x, give), (0, gp_o, own)):
        out[:, QKV] = dot_tn(normed[...], gp[...]).astype(BF)
        out[:, OUT] = dot_tn(mixed[...], grad_attn[:, place(core, side, 0, 384)]).astype(BF)
        out[:, SMALL] = small[...].astype(BF)


def dense_grads(normed, gp_o, gp_x, mixed, grad_attn, small):
    core = lax.axis_index("core").astype(jnp.int32).reshape(1)
    tokens, width = normed.shape
    rows = 256
    cols = pl.BlockSpec((tokens, rows), lambda i: (0, i))
    whole = pl.BlockSpec(memory_space=pltpu.VMEM)
    block = pl.BlockSpec((rows, 1664), lambda i: (i, 0))
    return pl.pallas_call(
        dense_grad_kernel,
        grid=(width // rows,),
        in_specs=[
            pl.BlockSpec(memory_space=pltpu.SMEM), cols, whole, whole, cols, whole,
            pl.BlockSpec((rows, 128), lambda i: (i, 0)),
        ],
        out_specs=[block, block],
        out_shape=[jax.ShapeDtypeStruct((width, 1664), BF)] * 2,
        compiler_params=pltpu.CompilerParams(vmem_limit_bytes=VMEM),
        cost_estimate=pl.CostEstimate(flops=1 << 20, bytes_accessed=1 << 16, transcendentals=0),
    )(core, normed, gp_o, gp_x, mixed, grad_attn, small)


def forward_kernel(rows, w_in, w_out, hidden, slope, part):
    pre = dot(rows[...], w_in[0, 0])
    cdf, steep = gelu_parts(pre)
    hidden[...] = (pre * cdf).astype(BF)
    slope[...] = steep.astype(BF)
    part[...] = dot(hidden[...], w_out[0, 0]).astype(BF)


def backward_kernel(grows, slope, w_in, w_out, grad_pre, part):
    grad_hidden = dot_nt(grows[...], w_out[0, 0])
    grad_pre[...] = (grad_hidden * slope[...].astype(F32)).astype(BF)
    part[...] = dot_nt(grad_pre[...], w_in[0, 0]).astype(BF)


def both_kernel(rows, w_in, w_out, hidden, grad_pre, part):
    groups, _, slots, width = rows.shape
    pre = dot(rows[:, 0].reshape(groups * slots, width), w_in[0, 0])
    cdf, steep = gelu_parts(pre)
    hidden[...] = (pre * cdf).astype(BF)
    out = dot(hidden[...], w_out[0, 0]).astype(BF)
    part[:, 0] = out.reshape(groups, slots, width)
    grad_hidden = dot_nt(rows[:, 1].reshape(groups * slots, width), w_out[0, 0])
    grad_pre[...] = (grad_hidden * steep).astype(BF)
    out = dot_nt(grad_pre[...], w_in[0, 0]).astype(BF)
    part[:, 1] = out.reshape(groups, slots, width)


GROUPS = 32


def expert_call(kernel, depth, row_args, weights, out_dims, products):
    def spec(shape):
        block = (GROUPS * SLOTS,) + shape[1:] if len(shape) == 2 else (GROUPS,) + shape[1:]
        return pl.BlockSpec(block, lambda i: (i,) + (0,) * (len(shape) - 1))

    hidden_units, width = weights[1].shape[2:]
    count = row_args[-1].shape[0] * (1 if row_args[-1].ndim == 2 else SLOTS)
    moved = count * width * (len(row_args) + len(out_dims)) + 2 * hidden_units * width
    return pl.pallas_call(
        kernel,
        grid=(count // (GROUPS * SLOTS),),
        in_specs=[spec(a.shape) for a in row_args]
        + [pl.BlockSpec((1,) + w.shape[1:], lambda i: (depth, 0, 0, 0)) for w in weights],
        out_specs=[spec(shape) for shape in out_dims],
        out_shape=[jax.ShapeDtypeStruct(shape, BF) for shape in out_dims],
        compiler_params=pltpu.CompilerParams(vmem_limit_bytes=VMEM),
        cost_estimate=pl.CostEstimate(
            flops=2 * count * hidden_units * width * products,
            bytes_accessed=2 * moved,
            transcendentals=0,
        ),
    )(*row_args, *weights)


def join_cores(part_own, part_other):
    return (part_own.astype(F32) + swap_core(part_other).astype(F32)).astype(BF)


def routing(chosen, experts):
    flat = jnp.concatenate([chosen[:, 0], chosen[:, 1]])
    onehot = flat[:, None] == jnp.arange(experts, dtype=jnp.int32)[None, :]
    pairs = flat.shape[0]
    earlier = (
        lax.broadcasted_iota(jnp.int32, (pairs, pairs), 1)
        < lax.broadcasted_iota(jnp.int32, (pairs, pairs), 0)
    ).astype(BF)
    onehot = onehot.astype(F32)
    before = dot(earlier, onehot.astype(BF))
    position = jnp.sum(before * onehot, axis=1).astype(jnp.int32)
    return onehot, flat * SLOTS + position


def slot_codes(slots, kinds, dims, axis):
    row = lax.broadcasted_iota(jnp.int32, dims, axis)
    run = row // SLOTS
    return lax.rem(run, kinds), (run // (2 * kinds)) * SLOTS + lax.rem(row, SLOTS)


def one_hots(code, slots, kinds, kind):
    pairs = code.shape[0]
    found = []
    for dims, axis, codes in (((slots, pairs), 0, code[None, :]), ((pairs, slots), 1, code[:, None])):
        kind_of, slot_of = slot_codes(slots, kinds, dims, axis)
        found.append(((slot_of == codes) & (kind_of == kind)).astype(BF))
    return found


def router_forward(logits, onehot):
    router = jax.nn.softmax(logits, axis=-1)
    tokens = router.shape[0]
    gate = [
        jnp.sum(onehot[j * tokens : (j + 1) * tokens] * router, axis=1, keepdims=True)
        for j in range(2)
    ]
    return router, gate


def router_back(grad, picked, router, onehot, normed_two, router_w):
    tokens = router.shape[0]
    grad_router = 0.0
    for j in range(2):
        part = jnp.sum(grad * picked[j], axis=1, keepdims=True)
        grad_router = grad_router + onehot[j * tokens : (j + 1) * tokens] * part
    grad_logit = router * (grad_router - jnp.sum(grad_router * router, axis=-1, keepdims=True))
    grad_normed = jnp.dot(grad_logit, router_w.astype(F32).T, precision=HIGH)
    grad_router_w = jnp.dot(normed_two.astype(F32).T, grad_logit, precision=HIGH)
    return grad_normed, grad_router_w


def small_grads(grad_router_w, stats):
    return pad_cols(jnp.concatenate([grad_router_w, stats.T], axis=1), 128)


def per_device(
    image_tokens,
    cotangent,
    routes,
    norm_gains,
    norm_biases,
    qkv_weight,
    out_weight,
    router_weight,
    expert_in,
    expert_out,
):
    tokens, width = image_tokens.shape
    experts = lax.axis_size("ea")
    mine = []
    for b in range(LAYERS):
        small = jnp.concatenate([router_weight[b], norm_gains[b].T, norm_biases[b].T], axis=1)
        mine.append(core_dense(qkv_weight[b], out_weight[b], pad_cols(small, 128)))
    dense0 = split_dense(gather_cols(mine[0]))
    weights = [expert_in, expert_out]
    onehot0, code = routing(routes[0], experts)
    send, fetch = one_hots(code, experts * 2 * SLOTS, 1, 0)
    onehot1, code = routing(routes[1], experts)
    send_rows, fetch_rows = one_hots(code, experts * 4 * SLOTS, 2, 0)
    send_grads, fetch_grads = one_hots(code, experts * 4 * SLOTS, 2, 1)
    send_rows = send_rows[:, :tokens] + send_rows[:, tokens:]
    fetch_grads = fetch_grads[:tokens] + fetch_grads[tokens:]
    send1 = jnp.concatenate([send_rows, send_grads], axis=1)
    fetch1 = jnp.concatenate([fetch_rows, fetch_grads], axis=0)

    state = image_tokens.astype(F32)
    after0, normed0, logits, kept0 = attention(state, dense0)
    router0, gate0 = router_forward(logits[:, :experts], onehot0)
    arrived = exchange(dot(send[:, :tokens] + send[:, tokens:], normed0).astype(BF))
    gathered1 = gather_cols(mine[1], after=arrived)
    rows0 = (arrived, swap_core(arrived))
    first = [
        expert_call(forward_kernel, 0, [r], weights, [r.shape] * 3, 2) for r in rows0
    ]
    hidden0, slope0, part = zip(*first)
    returned = exchange(join_cores(*part))
    dense1 = split_dense(gathered1)
    picked = dot(fetch, returned)
    picked0 = (picked[:tokens], picked[tokens:])
    state1 = after0 + gate0[0] * picked0[0] + gate0[1] * picked0[1]

    grad = cotangent.astype(F32)
    after1, normed1, logits, kept1 = attention(state1, dense1)
    router1, gate1 = router_forward(logits[:, :experts], onehot1)
    rows = jnp.concatenate([normed1] + [(g * grad).astype(BF) for g in gate1], axis=0)
    arrived = exchange(dot(send1, rows).astype(BF)).reshape(-1, 2, SLOTS, width)
    both = (arrived, swap_core(arrived))
    flat = (arrived.shape[0] * SLOTS, width)
    second = [
        expert_call(both_kernel, 1, [r], weights, [flat, flat, r.shape], 4) for r in both
    ]
    hidden1, grad_pre1, part = zip(*second)
    returned = exchange(join_cores(*part).reshape(-1, width))
    grad_w_out1 = sum(dot_tn(h, r[:, 1].reshape(flat)) for h, r in zip(hidden1, both))
    grad_w_in1 = sum(dot_tn(r[:, 0].reshape(flat), g) for r, g in zip(both, grad_pre1))
    returned, grad_w_out1, grad_w_in1 = lax.optimization_barrier(
        (returned, grad_w_out1, grad_w_in1)
    )
    picked = dot(fetch1, returned)
    picked1 = (picked[:tokens], picked[tokens : 2 * tokens])
    grad_sent = picked[2 * tokens :]
    block_out = (after1 + gate1[0] * picked1[0] + gate1[1] * picked1[1]).astype(BF)

    extra, grad_router_w1 = router_back(
        grad, picked1, router1, onehot1, normed1, dense1[0][:, 1536 : 1536 + experts]
    )
    grad, stats1, terms1 = attention_back(grad, grad_sent + extra, kept1, dense1)

    grad_rows = jnp.concatenate([(g * grad).astype(BF) for g in gate0], axis=0)
    arrived = exchange(dot(send, grad_rows).astype(BF))
    pair1 = sum_send(*dense_grads(*terms1, small_grads(grad_router_w1, stats1)))
    grows0 = (arrived, swap_core(arrived))
    third = [
        expert_call(backward_kernel, 0, [r, s], weights, [r.shape] * 2, 2)
        for r, s in zip(grows0, slope0)
    ]
    grad_pre0, part = zip(*third)
    returned = exchange(join_cores(*part))
    returned, pair1 = lax.optimization_barrier((returned, pair1))
    parts1 = sum_exchange(pair1)
    picked = dot(fetch, returned)
    grad_sent = picked[:tokens] + picked[tokens:]
    extra, grad_router_w0 = router_back(
        grad, picked0, router0, onehot0, normed0, dense0[0][:, 1536 : 1536 + experts]
    )
    grad, stats0, terms0 = attention_back(grad, grad_sent + extra, kept0, dense0)
    grads0, parts1 = lax.optimization_barrier(
        (dense_grads(*terms0, small_grads(grad_router_w0, stats0)), parts1)
    )
    pair0 = sum_send(*grads0)
    parts0 = sum_exchange(pair0)
    (hidden0, grows0, rows0, grad_pre0), _ = lax.optimization_barrier(
        ((hidden0, grows0, rows0, grad_pre0), pair0)
    )
    grad_w_out0 = sum(dot_tn(h, g) for h, g in zip(hidden0, grows0))
    grad_w_in0 = sum(dot_tn(r, g) for r, g in zip(rows0, grad_pre0))
    (grad_w_out0, grad_w_in0), parts1 = lax.optimization_barrier(
        ((grad_w_out0, grad_w_in0), parts1)
    )
    sums1 = sum_finish(parts1)
    sums0 = sum_finish(parts0)

    qkv_sum, out_sum, small = (jnp.stack(pair) for pair in zip(sums0, sums1))
    return (
        block_out,
        grad,
        small[:, :, experts : experts + 2].transpose(0, 2, 1),
        small[:, :, experts + 2 : experts + 4].transpose(0, 2, 1),
        qkv_sum,
        out_sum,
        small[:, :, :experts],
        jnp.stack([grad_w_in0, grad_w_in1])[:, None],
        jnp.stack([grad_w_out0, grad_w_out1])[:, None],
    )


def solution(mesh):
    fine = Mesh(
        mesh.devices.reshape(mesh.shape["ea"], mesh.shape["row"] // 2, 2), ("ea", "half", "core")
    )
    row = ("half", "core")
    every = ("ea",) + row
    in_specs = (
        P(every, None),
        P(every, None),
        P(None, every, None),
        P(None, None, "ea"),
        P(None, None, "ea"),
        P(None, "ea", None),
        P(None, "ea", None),
        P(None, "ea", None),
        P(None, "ea", None, row),
        P(None, "ea", row, None),
    )
    out_specs = (
        P(every, None),
        P(every, None),
        P(None, None, "ea"),
        P(None, None, "ea"),
        P(None, "ea", None),
        P(None, "ea", None),
        P(None, "ea", None),
        P(None, "ea", None, row),
        P(None, "ea", row, None),
    )
    return jax.shard_map(
        per_device, mesh=fine, in_specs=in_specs, out_specs=out_specs, check_vma=False
    )
```

```python
import functools

import jax
import jax.numpy as jnp
from jax import lax
from jax.experimental import pallas as pl
from jax.experimental.pallas import tpu as pltpu
from jax.sharding import Mesh
from jax.sharding import PartitionSpec as P

HEADS = 12
HEAD = 64
SEQ = 197
LAYERS = 2
EPS = 1e-06
HIGH = lax.Precision.HIGHEST
BF = jnp.bfloat16
F32 = jnp.float32
SLOTS = 16
SCALE = HEAD ** (-0.5)
GROUP = ("ea", "half")
VMEM = 28 * 1024 * 1024


def dot(a, b, dims=((1,), (0,))):
    return lax.dot_general(a, b, (dims, ((), ())), preferred_element_type=F32)


def dot_nt(a, b):
    return dot(a, b, ((1,), (1,)))


def dot_tn(a, b):
    return dot(a, b, ((0,), (0,)))


def swap_core(value):
    return lax.ppermute(value, "core", [(0, 1), (1, 0)])


def exchange(rows):
    return lax.all_to_all(rows, GROUP, split_axis=0, concat_axis=0, tiled=True)


def gelu_parts(x):
    base = 1.0 + (0.3275911 * 0.7071067811865476) * jnp.abs(x)
    t = pl.reciprocal(base, approx=True)
    t = t * (2.0 - base * t)
    bell = jnp.exp2((x * x) * (-0.5 * 1.4426950408889634))
    poly = t * (
        0.5 * 0.254829592
        + t
        * (
            0.5 * -0.284496736
            + t * (0.5 * 1.421413741 + t * (0.5 * -1.453152027 + t * (0.5 * 1.061405429)))
        )
    )
    tail = poly * bell
    cdf = jnp.where(x < 0, tail, 1.0 - tail)
    return cdf, cdf + x * (bell * 0.3989422804014327)


def normalize(x, gain, bias):
    center = jnp.mean(x, axis=-1, keepdims=True)
    shifted = x - center
    spread = jnp.mean(shifted * shifted, axis=-1, keepdims=True)
    inv = lax.rsqrt(spread + EPS)
    unit = shifted * inv
    return unit * gain + bias, unit, inv


def normalize_back(grad, unit, inv, gain):
    scaled = grad * gain
    mean_a = jnp.mean(scaled, axis=-1, keepdims=True)
    mean_b = jnp.mean(scaled * unit, axis=-1, keepdims=True)
    return (
        inv * (scaled - mean_a - unit * mean_b),
        jnp.sum(grad * unit, axis=0),
        jnp.sum(grad, axis=0),
    )


def heads_of(matrix):
    return matrix.reshape(SEQ, HEADS, HEAD)


def gather_cols(mine, after=None):
    groups = lax.axis_size("ea")
    sent = jnp.broadcast_to(mine[None], (groups,) + mine.shape)
    if after is not None:
        sent, _ = lax.optimization_barrier((sent, after))
    got = lax.all_to_all(sent, "ea", split_axis=0, concat_axis=0)
    return got.reshape(-1, mine.shape[1])


def core_half(value, which=0):
    n = value.shape[1] // 2
    core = lax.axis_index("core")
    return lax.dynamic_slice_in_dim(value, (core if which == 0 else 1 - core) * n, n, 1)


def in_order(own, other):
    first = lax.axis_index("core") == 0
    return jnp.concatenate(
        [jnp.where(first, own, other), jnp.where(first, other, own)], axis=1
    )


def thirds(value):
    n = value.shape[1] // 3
    return [value[:, i * n : (i + 1) * n] for i in range(3)]


def core_dense(qkv, out, small):
    return jnp.concatenate([core_half(part) for part in thirds(qkv)] + [core_half(out), small], axis=1)


def split_dense(own):
    return own, swap_core(own)


def sum_send(own, give):
    return (own.astype(F32) + swap_core(give).astype(F32)).astype(BF)


def sum_exchange(pair):
    groups = lax.axis_size("ea")
    return lax.all_to_all(
        pair.reshape(groups, -1, pair.shape[1]), "ea", split_axis=0, concat_axis=0
    )


def swap_row(value, flip):
    return lax.ppermute(value, ("half", "core"), [(i, i ^ flip) for i in range(4)])


def sum_finish(*parts):
    part = jnp.concatenate([jnp.sum(p.astype(F32), axis=0) for p in parts], axis=1).astype(BF)
    full = part.astype(F32) + swap_row(part, 2).astype(F32)
    dense = part[:, :1536]
    other = swap_row(dense, 1).astype(F32) + swap_row(dense, 3).astype(F32)
    qkv = [
        in_order(own, more) for own, more in zip(thirds(full[:, :1152]), thirds(other[:, :1152]))
    ]
    return (
        jnp.concatenate(qkv, axis=1),
        in_order(full[:, 1152:1536], other[:, 1152:]),
        full[:, 1536:],
    )


def pad_cols(value, cols):
    return jnp.pad(value, ((0, 0), (0, cols - value.shape[1])))


def softmax_rows(scores):
    expo = jnp.exp(scores - jnp.max(scores, axis=-1, keepdims=True))
    return expo * (1.0 / jnp.sum(expo, axis=-1, keepdims=True))


def place(core, side, start, size):
    half = core if side == 0 else 1 - core
    return pl.ds(pl.multiple_of(half * 384 + start, 128), size)


def masked(pair, j):
    lane = lax.broadcasted_iota(jnp.int32, pair.shape, 1)
    return jnp.where((lane < HEAD) == (j == 0), pair, jnp.zeros_like(pair))


def merge(first, second):
    lane = lax.broadcasted_iota(jnp.int32, first.shape, 1)
    return jnp.where(lane < HEAD, first, second)


QKV = slice(0, 1152)
OUT = slice(1152, 1536)
SMALL = slice(1536, 1664)


def norms_of(own, experts):
    return own[:, SMALL].astype(F32).T[experts : experts + 4]


def attend_kernel(
    experts, core_ref, state, own, other, proj_o, proj_x, mixed, after, normed_two, logits, normed
):
    core = core_ref[0]
    norms = norms_of(own, experts)
    wide, _, _ = normalize(state[...], norms[0:1], norms[2:3])
    normed[...] = wide.astype(BF)
    for side, weight, proj in ((0, own, proj_o), (1, other, proj_x)):
        proj[...] = dot(normed[...], weight[:, QKV]).astype(BF)
        for at in range(0, 384, 128):
            query, key_part, value_part = (proj[:, i * 384 + at : i * 384 + at + 128] for i in range(3))
            found = []
            for j in range(2):
                shares = softmax_rows(dot_nt(masked(query, j), key_part) * SCALE)
                found.append(dot(shares.astype(BF), value_part))
            mixed[:, place(core, side, at, 128)] = merge(*found).astype(BF)
    for side, weight in ((0, own), (1, other)):
        cols = place(core, side, 0, 384)
        after[:, cols] = state[:, cols] + dot(mixed[...], weight[:, OUT])
    wide, _, _ = normalize(after[...], norms[1:2], norms[3:4])
    normed_two[...] = wide.astype(BF)
    logits[...] = dot(normed_two[...], own[:, SMALL])


def attend_back_kernel(
    experts, core_ref, grad, grad_two, state, after, proj_o, proj_x, mixed, small, own, other,
    grad_in, sum_o, sum_x, grad_attn, grad_mixed, gp_o, gp_x, normed, stats,
):
    core = core_ref[0]
    norms = norms_of(own, experts)
    _, unit, inv = normalize(after[...], norms[1:2], norms[3:4])
    part, gain_two, bias_two = normalize_back(grad_two[...], unit, inv, norms[1:2])
    grad_in[...] = grad[...] + part
    grad_attn[...] = grad_in[...].astype(BF)
    grad_mixed[...] = sum(
        dot_nt(grad_attn[:, place(core, side, 0, 384)], weight[:, OUT])
        for side, weight in ((0, own), (1, other))
    ).astype(BF)
    for side, proj, gp in ((0, proj_o, gp_o), (1, proj_x, gp_x)):
        for at in range(0, 384, 128):
            query, key_part, value_part = (proj[:, i * 384 + at : i * 384 + at + 128] for i in range(3))
            outer = grad_mixed[:, place(core, side, at, 128)]
            found = []
            for j in range(2):
                shares = softmax_rows(dot_nt(masked(query, j), key_part) * SCALE)
                grad_shares = dot_nt(masked(outer, j), value_part)
                inner = jnp.sum(grad_shares * shares, axis=-1, keepdims=True)
                raw = (shares * (grad_shares - inner) * SCALE).astype(BF)
                found.append(
                    (dot(raw, key_part), dot_tn(raw, query), dot_tn(shares.astype(BF), outer))
                )
            for i in range(3):
                gp[:, i * 384 + at : i * 384 + at + 128] = merge(found[0][i], found[1][i]).astype(BF)
    grad_normed = dot_nt(gp_o[...], own[:, QKV]) + dot_nt(gp_x[...], other[:, QKV])
    wide, unit, inv = normalize(state[...], norms[0:1], norms[2:3])
    normed[...] = wide.astype(BF)
    part, gain_one, bias_one = normalize_back(grad_normed, unit, inv, norms[0:1])
    grad_in[...] = grad_in[...] + part
    stats[...] = jnp.zeros_like(stats)
    for i, row in enumerate((gain_one, gain_two, bias_one, bias_two)):
        stats[experts + i : experts + i + 1, :] = row[None, :]
    narrow = (stats[...].T + small[...]).astype(BF)
    for side, gp, out in ((1, gp_x, sum_x), (0, gp_o, sum_o)):
        for at in range(0, 768, 256):
            rows = slice(at, at + 256)
            out[rows, QKV] = dot_tn(normed[:, rows], gp[...]).astype(BF)
            out[rows, OUT] = dot_tn(mixed[:, rows], grad_attn[:, place(core, side, 0, 384)]).astype(BF)
        out[:, SMALL] = narrow


def whole_call(kernel, args, outs, flops, scratch=()):
    core = lax.axis_index("core").astype(jnp.int32).reshape(1)
    vmem = pl.BlockSpec(memory_space=pltpu.VMEM)
    return pl.pallas_call(
        kernel,
        in_specs=[pl.BlockSpec(memory_space=pltpu.SMEM)] + [vmem] * len(args),
        out_specs=[vmem] * len(outs),
        out_shape=[jax.ShapeDtypeStruct(shape, kind) for shape, kind in outs],
        scratch_shapes=list(scratch),
        compiler_params=pltpu.CompilerParams(vmem_limit_bytes=VMEM + (12 << 20)),
        cost_estimate=pl.CostEstimate(flops=flops, bytes_accessed=8 << 20, transcendentals=0),
    )(core, *args)


def attention(state, dense):
    tokens, width = state.shape
    rows = lambda n, kind: ((tokens, n), kind)
    proj_o, proj_x, mixed, after, normed_two, logits = whole_call(
        functools.partial(attend_kernel, lax.axis_size("ea")),
        [state, *dense],
        [
            rows(1152, BF), rows(1152, BF), rows(width, BF), rows(width, F32), rows(width, BF),
            rows(128, F32),
        ],
        4 * tokens * width * (4 * width + 4 * tokens),
        [pltpu.VMEM((tokens, width), BF)],
    )
    return after, normed_two, logits, (state, proj_o, proj_x, mixed, after)


def attention_back(grad, grad_two, grad_router_w, kept, dense):
    state, proj_o, proj_x, mixed, after = kept
    tokens, width = grad.shape
    rows = lambda n, kind: ((tokens, n), kind)
    scratch = [rows(width, BF), rows(width, BF), rows(1152, BF), rows(1152, BF), rows(width, BF)]
    grad_in, sum_o, sum_x = whole_call(
        functools.partial(attend_back_kernel, lax.axis_size("ea")),
        [grad, grad_two, state, after, proj_o, proj_x, mixed, pad_cols(grad_router_w, 128), *dense],
        [rows(width, F32), ((width, 1664), BF), ((width, 1664), BF)],
        12 * tokens * width * (4 * width + 8 * tokens),
        [pltpu.VMEM(*dims) for dims in scratch + [((128, width), F32)]],
    )
    return grad_in, (sum_o, sum_x)


def forward_kernel(rows, w_in, w_out, hidden, slope, part):
    pre = dot(rows[...], w_in[0, 0])
    cdf, steep = gelu_parts(pre)
    hidden[...] = (pre * cdf).astype(BF)
    slope[...] = steep.astype(BF)
    part[...] = dot(hidden[...], w_out[0, 0]).astype(BF)


def backward_kernel(grows, slope, w_in, w_out, grad_pre, part):
    grad_hidden = dot_nt(grows[...], w_out[0, 0])
    grad_pre[...] = (grad_hidden * slope[...].astype(F32)).astype(BF)
    part[...] = dot_nt(grad_pre[...], w_in[0, 0]).astype(BF)


def both_kernel(rows, w_in, w_out, hidden, grad_pre, part):
    groups, _, slots, width = rows.shape
    pre = dot(rows[:, 0].reshape(groups * slots, width), w_in[0, 0])
    cdf, steep = gelu_parts(pre)
    hidden[...] = (pre * cdf).astype(BF)
    out = dot(hidden[...], w_out[0, 0]).astype(BF)
    part[:, 0] = out.reshape(groups, slots, width)
    grad_hidden = dot_nt(rows[:, 1].reshape(groups * slots, width), w_out[0, 0])
    grad_pre[...] = (grad_hidden * steep).astype(BF)
    out = dot_nt(grad_pre[...], w_in[0, 0]).astype(BF)
    part[:, 1] = out.reshape(groups, slots, width)


GROUPS = 32


def expert_call(kernel, depth, row_args, weights, out_dims, products):
    def spec(shape):
        block = (GROUPS * SLOTS,) + shape[1:] if len(shape) == 2 else (GROUPS,) + shape[1:]
        return pl.BlockSpec(block, lambda i: (i,) + (0,) * (len(shape) - 1))

    hidden_units, width = weights[1].shape[2:]
    count = row_args[-1].shape[0] * (1 if row_args[-1].ndim == 2 else SLOTS)
    moved = count * width * (len(row_args) + len(out_dims)) + 2 * hidden_units * width
    return pl.pallas_call(
        kernel,
        grid=(count // (GROUPS * SLOTS),),
        in_specs=[spec(a.shape) for a in row_args]
        + [pl.BlockSpec((1,) + w.shape[1:], lambda i: (depth, 0, 0, 0)) for w in weights],
        out_specs=[spec(shape) for shape in out_dims],
        out_shape=[jax.ShapeDtypeStruct(shape, BF) for shape in out_dims],
        compiler_params=pltpu.CompilerParams(vmem_limit_bytes=VMEM),
        cost_estimate=pl.CostEstimate(
            flops=2 * count * hidden_units * width * products,
            bytes_accessed=2 * moved,
            transcendentals=0,
        ),
    )(*row_args, *weights)


def join_cores(part_own, part_other):
    return (part_own.astype(F32) + swap_core(part_other).astype(F32)).astype(BF)


def routing(chosen, experts):
    flat = jnp.concatenate([chosen[:, 0], chosen[:, 1]])
    onehot = flat[:, None] == jnp.arange(experts, dtype=jnp.int32)[None, :]
    pairs = flat.shape[0]
    earlier = (
        lax.broadcasted_iota(jnp.int32, (pairs, pairs), 1)
        < lax.broadcasted_iota(jnp.int32, (pairs, pairs), 0)
    ).astype(BF)
    onehot = onehot.astype(F32)
    before = dot(earlier, onehot.astype(BF))
    position = jnp.sum(before * onehot, axis=1).astype(jnp.int32)
    return onehot, flat * SLOTS + position


def slot_codes(slots, kinds, dims, axis):
    row = lax.broadcasted_iota(jnp.int32, dims, axis)
    run = row // SLOTS
    return lax.rem(run, kinds), (run // (2 * kinds)) * SLOTS + lax.rem(row, SLOTS)


def one_hots(code, slots, kinds, kind):
    pairs = code.shape[0]
    found = []
    for dims, axis, codes in (((slots, pairs), 0, code[None, :]), ((pairs, slots), 1, code[:, None])):
        kind_of, slot_of = slot_codes(slots, kinds, dims, axis)
        found.append(((slot_of == codes) & (kind_of == kind)).astype(BF))
    return found


def router_forward(logits, onehot):
    router = jax.nn.softmax(logits, axis=-1)
    tokens = router.shape[0]
    gate = [
        jnp.sum(onehot[j * tokens : (j + 1) * tokens] * router, axis=1, keepdims=True)
        for j in range(2)
    ]
    return router, gate


def router_back(grad, picked, router, onehot, normed_two, router_w):
    tokens = router.shape[0]
    grad_router = 0.0
    for j in range(2):
        part = jnp.sum(grad * picked[j], axis=1, keepdims=True)
        grad_router = grad_router + onehot[j * tokens : (j + 1) * tokens] * part
    grad_logit = router * (grad_router - jnp.sum(grad_router * router, axis=-1, keepdims=True))
    grad_normed = jnp.dot(grad_logit, router_w.astype(F32).T, precision=HIGH)
    grad_router_w = jnp.dot(normed_two.astype(F32).T, grad_logit, precision=HIGH)
    return grad_normed, grad_router_w


def per_device(
    image_tokens,
    cotangent,
    routes,
    norm_gains,
    norm_biases,
    qkv_weight,
    out_weight,
    router_weight,
    expert_in,
    expert_out,
):
    tokens, width = image_tokens.shape
    experts = lax.axis_size("ea")
    mine = []
    for b in range(LAYERS):
        small = jnp.concatenate([router_weight[b], norm_gains[b].T, norm_biases[b].T], axis=1)
        mine.append(core_dense(qkv_weight[b], out_weight[b], pad_cols(small, 128)))
    dense0 = split_dense(gather_cols(mine[0]))
    weights = [expert_in, expert_out]
    onehot0, code = routing(routes[0], experts)
    send, fetch = one_hots(code, experts * 2 * SLOTS, 1, 0)
    onehot1, code = routing(routes[1], experts)
    send_rows, fetch_rows = one_hots(code, experts * 4 * SLOTS, 2, 0)
    send_grads, fetch_grads = one_hots(code, experts * 4 * SLOTS, 2, 1)
    send_rows = send_rows[:, :tokens] + send_rows[:, tokens:]
    fetch_grads = fetch_grads[:tokens] + fetch_grads[tokens:]
    send1 = jnp.concatenate([send_rows, send_grads], axis=1)
    fetch1 = jnp.concatenate([fetch_rows, fetch_grads], axis=0)

    state = image_tokens.astype(F32)
    after0, normed0, logits, kept0 = attention(state, dense0)
    router0, gate0 = router_forward(logits[:, :experts], onehot0)
    arrived = exchange(dot(send[:, :tokens] + send[:, tokens:], normed0).astype(BF))
    gathered1 = gather_cols(mine[1], after=arrived)
    rows0 = (arrived, swap_core(arrived))
    first = [
        expert_call(forward_kernel, 0, [r], weights, [r.shape] * 3, 2) for r in rows0
    ]
    hidden0, slope0, part = zip(*first)
    returned = exchange(join_cores(*part))
    dense1 = split_dense(gathered1)
    picked = dot(fetch, returned)
    picked0 = (picked[:tokens], picked[tokens:])
    state1 = after0 + gate0[0] * picked0[0] + gate0[1] * picked0[1]

    grad = cotangent.astype(F32)
    after1, normed1, logits, kept1 = attention(state1, dense1)
    router1, gate1 = router_forward(logits[:, :experts], onehot1)
    rows = jnp.concatenate([normed1] + [(g * grad).astype(BF) for g in gate1], axis=0)
    arrived = exchange(dot(send1, rows).astype(BF)).reshape(-1, 2, SLOTS, width)
    both = (arrived, swap_core(arrived))
    flat = (arrived.shape[0] * SLOTS, width)
    second = [
        expert_call(both_kernel, 1, [r], weights, [flat, flat, r.shape], 4) for r in both
    ]
    hidden1, grad_pre1, part = zip(*second)
    returned = exchange(join_cores(*part).reshape(-1, width))
    grad_w_out1 = sum(dot_tn(h, r[:, 1].reshape(flat)) for h, r in zip(hidden1, both))
    grad_w_in1 = sum(dot_tn(r[:, 0].reshape(flat), g) for r, g in zip(both, grad_pre1))
    returned, grad_w_out1, grad_w_in1 = lax.optimization_barrier(
        (returned, grad_w_out1, grad_w_in1)
    )
    picked = dot(fetch1, returned)
    picked1 = (picked[:tokens], picked[tokens : 2 * tokens])
    grad_sent = picked[2 * tokens :]
    block_out = (after1 + gate1[0] * picked1[0] + gate1[1] * picked1[1]).astype(BF)

    extra, grad_router_w1 = router_back(
        grad, picked1, router1, onehot1, normed1, dense1[0][:, 1536 : 1536 + experts]
    )
    grad, grads1 = attention_back(grad, grad_sent + extra, grad_router_w1, kept1, dense1)

    grad_rows = jnp.concatenate([(g * grad).astype(BF) for g in gate0], axis=0)
    arrived = exchange(dot(send, grad_rows).astype(BF))
    pair1 = sum_send(*grads1)
    arrived, pair1 = lax.optimization_barrier((arrived, pair1))
    parts1a = sum_exchange(pair1[:, :768])
    grows0 = (arrived, swap_core(arrived))
    third = [
        expert_call(backward_kernel, 0, [r, s], weights, [r.shape] * 2, 2)
        for r, s in zip(grows0, slope0)
    ]
    grad_pre0, part = zip(*third)
    back, parts1a = lax.optimization_barrier((join_cores(*part), parts1a))
    returned = exchange(back)
    returned, pair1 = lax.optimization_barrier((returned, pair1))
    parts1b = sum_exchange(pair1[:, 768:])
    picked = dot(fetch, returned)
    grad_sent = picked[:tokens] + picked[tokens:]
    extra, grad_router_w0 = router_back(
        grad, picked0, router0, onehot0, normed0, dense0[0][:, 1536 : 1536 + experts]
    )
    grad, grads0 = attention_back(grad, grad_sent + extra, grad_router_w0, kept0, dense0)
    grads0, parts1b = lax.optimization_barrier((grads0, parts1b))
    pair0 = sum_send(*grads0)
    parts0 = sum_exchange(pair0)
    (hidden0, grows0, rows0, grad_pre0), _ = lax.optimization_barrier(
        ((hidden0, grows0, rows0, grad_pre0), pair0)
    )
    grad_w_out0 = sum(dot_tn(h, g) for h, g in zip(hidden0, grows0))
    grad_w_in0 = sum(dot_tn(r, g) for r, g in zip(rows0, grad_pre0))
    (grad_w_out0, grad_w_in0), parts1b = lax.optimization_barrier(
        ((grad_w_out0, grad_w_in0), parts1b)
    )
    sums1 = sum_finish(parts1a, parts1b)
    sums0 = sum_finish(parts0)

    qkv_sum, out_sum, small = (jnp.stack(pair) for pair in zip(sums0, sums1))
    return (
        block_out,
        grad,
        small[:, :, experts : experts + 2].transpose(0, 2, 1),
        small[:, :, experts + 2 : experts + 4].transpose(0, 2, 1),
        qkv_sum,
        out_sum,
        small[:, :, :experts],
        jnp.stack([grad_w_in0, grad_w_in1])[:, None],
        jnp.stack([grad_w_out0, grad_w_out1])[:, None],
    )


def solution(mesh):
    fine = Mesh(
        mesh.devices.reshape(mesh.shape["ea"], mesh.shape["row"] // 2, 2), ("ea", "half", "core")
    )
    row = ("half", "core")
    every = ("ea",) + row
    in_specs = (
        P(every, None),
        P(every, None),
        P(None, every, None),
        P(None, None, "ea"),
        P(None, None, "ea"),
        P(None, "ea", None),
        P(None, "ea", None),
        P(None, "ea", None),
        P(None, "ea", None, row),
        P(None, "ea", row, None),
    )
    out_specs = (
        P(every, None),
        P(every, None),
        P(None, None, "ea"),
        P(None, None, "ea"),
        P(None, "ea", None),
        P(None, "ea", None),
        P(None, "ea", None),
        P(None, "ea", None, row),
        P(None, "ea", row, None),
    )
    return jax.shard_map(
        per_device, mesh=fine, in_specs=in_specs, out_specs=out_specs, check_vma=False
    )
```

```python
import functools

import jax
import jax.numpy as jnp
from jax import lax
from jax.experimental import pallas as pl
from jax.experimental.pallas import tpu as pltpu
from jax.sharding import Mesh
from jax.sharding import PartitionSpec as P

HEADS = 12
HEAD = 64
SEQ = 197
LAYERS = 2
EPS = 1e-06
HIGH = lax.Precision.HIGHEST
BF = jnp.bfloat16
F32 = jnp.float32
SLOTS = 16
SCALE = HEAD ** (-0.5)
GROUP = ("ea", "half")
VMEM = 28 * 1024 * 1024


def dot(a, b, dims=((1,), (0,))):
    return lax.dot_general(a, b, (dims, ((), ())), preferred_element_type=F32)


def dot_nt(a, b):
    return dot(a, b, ((1,), (1,)))


def dot_tn(a, b):
    return dot(a, b, ((0,), (0,)))


def swap_core(value):
    return lax.ppermute(value, "core", [(0, 1), (1, 0)])


def exchange(rows):
    return lax.all_to_all(rows, GROUP, split_axis=0, concat_axis=0, tiled=True)


def gelu_parts(x):
    base = 1.0 + (0.3275911 * 0.7071067811865476) * jnp.abs(x)
    t = pl.reciprocal(base, approx=True)
    t = t * (2.0 - base * t)
    bell = jnp.exp2((x * x) * (-0.5 * 1.4426950408889634))
    poly = t * (
        0.5 * 0.254829592
        + t
        * (
            0.5 * -0.284496736
            + t * (0.5 * 1.421413741 + t * (0.5 * -1.453152027 + t * (0.5 * 1.061405429)))
        )
    )
    tail = poly * bell
    cdf = jnp.where(x < 0, tail, 1.0 - tail)
    return cdf, cdf + x * (bell * 0.3989422804014327)


def normalize(x, gain, bias):
    center = jnp.mean(x, axis=-1, keepdims=True)
    shifted = x - center
    spread = jnp.mean(shifted * shifted, axis=-1, keepdims=True)
    inv = lax.rsqrt(spread + EPS)
    unit = shifted * inv
    return unit * gain + bias, unit, inv


def normalize_back(grad, unit, inv, gain):
    scaled = grad * gain
    mean_a = jnp.mean(scaled, axis=-1, keepdims=True)
    mean_b = jnp.mean(scaled * unit, axis=-1, keepdims=True)
    return (
        inv * (scaled - mean_a - unit * mean_b),
        jnp.sum(grad * unit, axis=0),
        jnp.sum(grad, axis=0),
    )


def heads_of(matrix):
    return matrix.reshape(SEQ, HEADS, HEAD)


def gather_cols(mine, after=None):
    groups = lax.axis_size("ea")
    sent = jnp.broadcast_to(mine[None], (groups,) + mine.shape)
    if after is not None:
        sent, _ = lax.optimization_barrier((sent, after))
    got = lax.all_to_all(sent, "ea", split_axis=0, concat_axis=0)
    return got.reshape(-1, mine.shape[1])


def core_half(value, which=0):
    n = value.shape[1] // 2
    core = lax.axis_index("core")
    return lax.dynamic_slice_in_dim(value, (core if which == 0 else 1 - core) * n, n, 1)


def in_order(own, other):
    first = lax.axis_index("core") == 0
    return jnp.concatenate(
        [jnp.where(first, own, other), jnp.where(first, other, own)], axis=1
    )


def thirds(value):
    n = value.shape[1] // 3
    return [value[:, i * n : (i + 1) * n] for i in range(3)]


def core_dense(qkv, out, small):
    return jnp.concatenate([core_half(part) for part in thirds(qkv)] + [core_half(out), small], axis=1)


def split_dense(own):
    return own, swap_core(own)


def sum_send(own, give):
    return (own.astype(F32) + swap_core(give).astype(F32)).astype(BF)


def sum_exchange(pair):
    groups = lax.axis_size("ea")
    return lax.all_to_all(
        pair.reshape(groups, -1, pair.shape[1]), "ea", split_axis=0, concat_axis=0
    )


def swap_row(value, flip):
    return lax.ppermute(value, ("half", "core"), [(i, i ^ flip) for i in range(4)])


def sum_finish(*parts):
    blocks = len(parts)
    part = jnp.concatenate([jnp.sum(p.astype(F32), axis=0) for p in parts], axis=0).astype(BF)
    full = part.astype(F32) + swap_row(part, 2).astype(F32)
    dense = part[:, :1536]
    other = swap_row(dense, 1).astype(F32) + swap_row(dense, 3).astype(F32)
    qkv = [
        in_order(own, more) for own, more in zip(thirds(full[:, :1152]), thirds(other[:, :1152]))
    ]
    return [
        value.reshape(blocks, -1, value.shape[1])
        for value in (
            jnp.concatenate(qkv, axis=1),
            in_order(full[:, 1152:1536], other[:, 1152:]),
            full[:, 1536:],
        )
    ]


def pad_cols(value, cols):
    return jnp.pad(value, ((0, 0), (0, cols - value.shape[1])))


def softmax_rows(scores):
    expo = jnp.exp(scores - jnp.max(scores, axis=-1, keepdims=True))
    return expo * (1.0 / jnp.sum(expo, axis=-1, keepdims=True))


def place(core, side, start, size):
    half = core if side == 0 else 1 - core
    return pl.ds(pl.multiple_of(half * 384 + start, 128), size)


def masked(pair, j):
    lane = lax.broadcasted_iota(jnp.int32, pair.shape, 1)
    return jnp.where((lane < HEAD) == (j == 0), pair, jnp.zeros_like(pair))


def merge(first, second):
    lane = lax.broadcasted_iota(jnp.int32, first.shape, 1)
    return jnp.where(lane < HEAD, first, second)


QKV = slice(0, 1152)
OUT = slice(1152, 1536)
SMALL = slice(1536, 1664)


def norms_of(own, experts):
    return own[:, SMALL].astype(F32).T[experts : experts + 4]


def attend_kernel(
    experts, core_ref, state, own, other, proj_o, proj_x, mixed, after, normed_two, logits, normed
):
    core = core_ref[0]
    norms = norms_of(own, experts)
    wide, _, _ = normalize(state[...], norms[0:1], norms[2:3])
    normed[...] = wide.astype(BF)
    for side, weight, proj in ((0, own, proj_o), (1, other, proj_x)):
        proj[...] = dot(normed[...], weight[:, QKV]).astype(BF)
        for at in range(0, 384, 128):
            query, key_part, value_part = (proj[:, i * 384 + at : i * 384 + at + 128] for i in range(3))
            found = []
            for j in range(2):
                shares = softmax_rows(dot_nt(masked(query, j), key_part) * SCALE)
                found.append(dot(shares.astype(BF), value_part))
            mixed[:, place(core, side, at, 128)] = merge(*found).astype(BF)
    for side, weight in ((0, own), (1, other)):
        cols = place(core, side, 0, 384)
        after[:, cols] = state[:, cols] + dot(mixed[...], weight[:, OUT])
    wide, _, _ = normalize(after[...], norms[1:2], norms[3:4])
    normed_two[...] = wide.astype(BF)
    logits[...] = dot(normed_two[...], own[:, SMALL])


def attend_back_kernel(
    experts, core_ref, grad, grad_two, state, after, proj_o, proj_x, mixed, small, own, other,
    grad_in, sum_o, sum_x, grad_attn, grad_mixed, gp_o, gp_x, normed, stats,
):
    core = core_ref[0]
    norms = norms_of(own, experts)
    _, unit, inv = normalize(after[...], norms[1:2], norms[3:4])
    part, gain_two, bias_two = normalize_back(grad_two[...], unit, inv, norms[1:2])
    grad_in[...] = grad[...] + part
    grad_attn[...] = grad_in[...].astype(BF)
    grad_mixed[...] = sum(
        dot_nt(grad_attn[:, place(core, side, 0, 384)], weight[:, OUT])
        for side, weight in ((0, own), (1, other))
    ).astype(BF)
    for side, proj, gp in ((0, proj_o, gp_o), (1, proj_x, gp_x)):
        for at in range(0, 384, 128):
            query, key_part, value_part = (proj[:, i * 384 + at : i * 384 + at + 128] for i in range(3))
            outer = grad_mixed[:, place(core, side, at, 128)]
            found = []
            for j in range(2):
                shares = softmax_rows(dot_nt(masked(query, j), key_part) * SCALE)
                grad_shares = dot_nt(masked(outer, j), value_part)
                inner = jnp.sum(grad_shares * shares, axis=-1, keepdims=True)
                raw = (shares * (grad_shares - inner) * SCALE).astype(BF)
                found.append(
                    (dot(raw, key_part), dot_tn(raw, query), dot_tn(shares.astype(BF), outer))
                )
            for i in range(3):
                gp[:, i * 384 + at : i * 384 + at + 128] = merge(found[0][i], found[1][i]).astype(BF)
    grad_normed = dot_nt(gp_o[...], own[:, QKV]) + dot_nt(gp_x[...], other[:, QKV])
    wide, unit, inv = normalize(state[...], norms[0:1], norms[2:3])
    normed[...] = wide.astype(BF)
    part, gain_one, bias_one = normalize_back(grad_normed, unit, inv, norms[0:1])
    grad_in[...] = grad_in[...] + part
    stats[...] = jnp.zeros_like(stats)
    for i, row in enumerate((gain_one, gain_two, bias_one, bias_two)):
        stats[experts + i : experts + i + 1, :] = row[None, :]
    narrow = (stats[...].T + small[...]).astype(BF)
    for side, gp, out in ((1, gp_x, sum_x), (0, gp_o, sum_o)):
        for at in range(0, 768, 256):
            rows = slice(at, at + 256)
            out[rows, QKV] = dot_tn(normed[:, rows], gp[...]).astype(BF)
            out[rows, OUT] = dot_tn(mixed[:, rows], grad_attn[:, place(core, side, 0, 384)]).astype(BF)
        out[:, SMALL] = narrow


def whole_call(kernel, args, outs, flops, scratch=()):
    core = lax.axis_index("core").astype(jnp.int32).reshape(1)
    vmem = pl.BlockSpec(memory_space=pltpu.VMEM)
    return pl.pallas_call(
        kernel,
        in_specs=[pl.BlockSpec(memory_space=pltpu.SMEM)] + [vmem] * len(args),
        out_specs=[vmem] * len(outs),
        out_shape=[jax.ShapeDtypeStruct(shape, kind) for shape, kind in outs],
        scratch_shapes=list(scratch),
        compiler_params=pltpu.CompilerParams(vmem_limit_bytes=VMEM + (12 << 20)),
        cost_estimate=pl.CostEstimate(flops=flops, bytes_accessed=8 << 20, transcendentals=0),
    )(core, *args)


def attention(state, dense):
    tokens, width = state.shape
    rows = lambda n, kind: ((tokens, n), kind)
    proj_o, proj_x, mixed, after, normed_two, logits = whole_call(
        functools.partial(attend_kernel, lax.axis_size("ea")),
        [state, *dense],
        [
            rows(1152, BF), rows(1152, BF), rows(width, BF), rows(width, F32), rows(width, BF),
            rows(128, F32),
        ],
        4 * tokens * width * (4 * width + 4 * tokens),
        [pltpu.VMEM((tokens, width), BF)],
    )
    return after, normed_two, logits, (state, proj_o, proj_x, mixed, after)


def attention_back(grad, grad_two, grad_router_w, kept, dense):
    state, proj_o, proj_x, mixed, after = kept
    tokens, width = grad.shape
    rows = lambda n, kind: ((tokens, n), kind)
    scratch = [rows(width, BF), rows(width, BF), rows(1152, BF), rows(1152, BF), rows(width, BF)]
    grad_in, sum_o, sum_x = whole_call(
        functools.partial(attend_back_kernel, lax.axis_size("ea")),
        [grad, grad_two, state, after, proj_o, proj_x, mixed, pad_cols(grad_router_w, 128), *dense],
        [rows(width, F32), ((width, 1664), BF), ((width, 1664), BF)],
        12 * tokens * width * (4 * width + 8 * tokens),
        [pltpu.VMEM(*dims) for dims in scratch + [((128, width), F32)]],
    )
    return grad_in, (sum_o, sum_x)


def forward_kernel(rows, w_in, w_out, hidden, slope, part):
    pre = dot(rows[...], w_in[0, 0])
    cdf, steep = gelu_parts(pre)
    hidden[...] = (pre * cdf).astype(BF)
    slope[...] = steep.astype(BF)
    part[...] = dot(hidden[...], w_out[0, 0]).astype(BF)


def backward_kernel(grows, slope, w_in, w_out, grad_pre, part):
    grad_hidden = dot_nt(grows[...], w_out[0, 0])
    grad_pre[...] = (grad_hidden * slope[...].astype(F32)).astype(BF)
    part[...] = dot_nt(grad_pre[...], w_in[0, 0]).astype(BF)


def both_kernel(rows, w_in, w_out, hidden, grad_pre, part):
    groups, _, slots, width = rows.shape
    pre = dot(rows[:, 0].reshape(groups * slots, width), w_in[0, 0])
    cdf, steep = gelu_parts(pre)
    hidden[...] = (pre * cdf).astype(BF)
    out = dot(hidden[...], w_out[0, 0]).astype(BF)
    part[:, 0] = out.reshape(groups, slots, width)
    grad_hidden = dot_nt(rows[:, 1].reshape(groups * slots, width), w_out[0, 0])
    grad_pre[...] = (grad_hidden * steep).astype(BF)
    out = dot_nt(grad_pre[...], w_in[0, 0]).astype(BF)
    part[:, 1] = out.reshape(groups, slots, width)


GROUPS = 32


def expert_call(kernel, depth, row_args, weights, out_dims, products):
    def spec(shape):
        block = (GROUPS * SLOTS,) + shape[1:] if len(shape) == 2 else (GROUPS,) + shape[1:]
        return pl.BlockSpec(block, lambda i: (i,) + (0,) * (len(shape) - 1))

    hidden_units, width = weights[1].shape[2:]
    count = row_args[-1].shape[0] * (1 if row_args[-1].ndim == 2 else SLOTS)
    moved = count * width * (len(row_args) + len(out_dims)) + 2 * hidden_units * width
    return pl.pallas_call(
        kernel,
        grid=(count // (GROUPS * SLOTS),),
        in_specs=[spec(a.shape) for a in row_args]
        + [pl.BlockSpec((1,) + w.shape[1:], lambda i: (depth, 0, 0, 0)) for w in weights],
        out_specs=[spec(shape) for shape in out_dims],
        out_shape=[jax.ShapeDtypeStruct(shape, BF) for shape in out_dims],
        compiler_params=pltpu.CompilerParams(vmem_limit_bytes=VMEM),
        cost_estimate=pl.CostEstimate(
            flops=2 * count * hidden_units * width * products,
            bytes_accessed=2 * moved,
            transcendentals=0,
        ),
    )(*row_args, *weights)


def join_cores(part_own, part_other):
    return (part_own.astype(F32) + swap_core(part_other).astype(F32)).astype(BF)


def routing(chosen, experts):
    flat = jnp.concatenate([chosen[:, 0], chosen[:, 1]])
    onehot = flat[:, None] == jnp.arange(experts, dtype=jnp.int32)[None, :]
    pairs = flat.shape[0]
    earlier = (
        lax.broadcasted_iota(jnp.int32, (pairs, pairs), 1)
        < lax.broadcasted_iota(jnp.int32, (pairs, pairs), 0)
    ).astype(BF)
    onehot = onehot.astype(F32)
    before = dot(earlier, onehot.astype(BF))
    position = jnp.sum(before * onehot, axis=1).astype(jnp.int32)
    return onehot, flat * SLOTS + position


def slot_codes(slots, kinds, dims, axis):
    row = lax.broadcasted_iota(jnp.int32, dims, axis)
    run = row // SLOTS
    return lax.rem(run, kinds), (run // (2 * kinds)) * SLOTS + lax.rem(row, SLOTS)


def one_hots(code, slots, kinds, kind):
    pairs = code.shape[0]
    found = []
    for dims, axis, codes in (((slots, pairs), 0, code[None, :]), ((pairs, slots), 1, code[:, None])):
        kind_of, slot_of = slot_codes(slots, kinds, dims, axis)
        found.append(((slot_of == codes) & (kind_of == kind)).astype(BF))
    return found


def router_forward(logits, onehot):
    router = jax.nn.softmax(logits, axis=-1)
    tokens = router.shape[0]
    gate = [
        jnp.sum(onehot[j * tokens : (j + 1) * tokens] * router, axis=1, keepdims=True)
        for j in range(2)
    ]
    return router, gate


def router_back(grad, picked, router, onehot, normed_two, router_w):
    tokens = router.shape[0]
    grad_router = 0.0
    for j in range(2):
        part = jnp.sum(grad * picked[j], axis=1, keepdims=True)
        grad_router = grad_router + onehot[j * tokens : (j + 1) * tokens] * part
    grad_logit = router * (grad_router - jnp.sum(grad_router * router, axis=-1, keepdims=True))
    grad_normed = jnp.dot(grad_logit, router_w.astype(F32).T, precision=HIGH)
    grad_router_w = jnp.dot(normed_two.astype(F32).T, grad_logit, precision=HIGH)
    return grad_normed, grad_router_w


def per_device(
    image_tokens,
    cotangent,
    routes,
    norm_gains,
    norm_biases,
    qkv_weight,
    out_weight,
    router_weight,
    expert_in,
    expert_out,
):
    tokens, width = image_tokens.shape
    experts = lax.axis_size("ea")
    mine = []
    for b in range(LAYERS):
        small = jnp.concatenate([router_weight[b], norm_gains[b].T, norm_biases[b].T], axis=1)
        mine.append(core_dense(qkv_weight[b], out_weight[b], pad_cols(small, 128)))
    dense0 = split_dense(gather_cols(mine[0]))
    weights = [expert_in, expert_out]
    onehot0, code = routing(routes[0], experts)
    send, fetch = one_hots(code, experts * 2 * SLOTS, 1, 0)
    onehot1, code = routing(routes[1], experts)
    send_rows, fetch_rows = one_hots(code, experts * 4 * SLOTS, 2, 0)
    send_grads, fetch_grads = one_hots(code, experts * 4 * SLOTS, 2, 1)
    send_rows = send_rows[:, :tokens] + send_rows[:, tokens:]
    fetch_grads = fetch_grads[:tokens] + fetch_grads[tokens:]
    send1 = jnp.concatenate([send_rows, send_grads], axis=1)
    fetch1 = jnp.concatenate([fetch_rows, fetch_grads], axis=0)

    state = image_tokens.astype(F32)
    after0, normed0, logits, kept0 = attention(state, dense0)
    router0, gate0 = router_forward(logits[:, :experts], onehot0)
    arrived = exchange(dot(send[:, :tokens] + send[:, tokens:], normed0).astype(BF))
    gathered1 = gather_cols(mine[1], after=arrived)
    rows0 = (arrived, swap_core(arrived))
    first = [
        expert_call(forward_kernel, 0, [r], weights, [r.shape] * 3, 2) for r in rows0
    ]
    hidden0, slope0, part = zip(*first)
    back, gathered1 = lax.optimization_barrier((join_cores(*part), gathered1))
    returned = exchange(back)
    dense1 = split_dense(gathered1)
    picked = dot(fetch, returned)
    picked0 = (picked[:tokens], picked[tokens:])
    state1 = after0 + gate0[0] * picked0[0] + gate0[1] * picked0[1]

    grad = cotangent.astype(F32)
    after1, normed1, logits, kept1 = attention(state1, dense1)
    router1, gate1 = router_forward(logits[:, :experts], onehot1)
    rows = jnp.concatenate([normed1] + [(g * grad).astype(BF) for g in gate1], axis=0)
    arrived = exchange(dot(send1, rows).astype(BF)).reshape(-1, 2, SLOTS, width)
    both = (arrived, swap_core(arrived))
    flat = (arrived.shape[0] * SLOTS, width)
    second = [
        expert_call(both_kernel, 1, [r], weights, [flat, flat, r.shape], 4) for r in both
    ]
    hidden1, grad_pre1, part = zip(*second)
    returned = exchange(join_cores(*part).reshape(-1, width))
    grad_w_out1 = sum(dot_tn(h, r[:, 1].reshape(flat)) for h, r in zip(hidden1, both))
    grad_w_in1 = sum(dot_tn(r[:, 0].reshape(flat), g) for r, g in zip(both, grad_pre1))
    returned, grad_w_out1, grad_w_in1 = lax.optimization_barrier(
        (returned, grad_w_out1, grad_w_in1)
    )
    picked = dot(fetch1, returned)
    picked1 = (picked[:tokens], picked[tokens : 2 * tokens])
    grad_sent = picked[2 * tokens :]
    block_out = (after1 + gate1[0] * picked1[0] + gate1[1] * picked1[1]).astype(BF)

    extra, grad_router_w1 = router_back(
        grad, picked1, router1, onehot1, normed1, dense1[0][:, 1536 : 1536 + experts]
    )
    grad, grads1 = attention_back(grad, grad_sent + extra, grad_router_w1, kept1, dense1)

    grad_rows = jnp.concatenate([(g * grad).astype(BF) for g in gate0], axis=0)
    arrived = exchange(dot(send, grad_rows).astype(BF))
    pair1 = sum_send(*grads1)
    arrived, pair1 = lax.optimization_barrier((arrived, pair1))
    grows0 = (arrived, swap_core(arrived))
    third = [
        expert_call(backward_kernel, 0, [r, s], weights, [r.shape] * 2, 2)
        for r, s in zip(grows0, slope0)
    ]
    grad_pre0, part = zip(*third)
    returned = exchange(join_cores(*part))
    grad_w_out0 = sum(dot_tn(h, g) for h, g in zip(hidden0, grows0))
    grad_w_in0 = sum(dot_tn(r, g) for r, g in zip(rows0, grad_pre0))
    returned, pair1, grad_w_out0, grad_w_in0 = lax.optimization_barrier(
        (returned, pair1, grad_w_out0, grad_w_in0)
    )
    parts1 = sum_exchange(pair1)
    picked = dot(fetch, returned)
    grad_sent = picked[:tokens] + picked[tokens:]
    extra, grad_router_w0 = router_back(
        grad, picked0, router0, onehot0, normed0, dense0[0][:, 1536 : 1536 + experts]
    )
    grad, grads0 = attention_back(grad, grad_sent + extra, grad_router_w0, kept0, dense0)
    grads0, parts1 = lax.optimization_barrier((grads0, parts1))
    parts0 = sum_exchange(sum_send(*grads0))
    qkv_sum, out_sum, small = sum_finish(parts0, parts1)

    return (
        block_out,
        grad,
        small[:, :, experts : experts + 2].transpose(0, 2, 1),
        small[:, :, experts + 2 : experts + 4].transpose(0, 2, 1),
        qkv_sum,
        out_sum,
        small[:, :, :experts],
        jnp.stack([grad_w_in0, grad_w_in1])[:, None],
        jnp.stack([grad_w_out0, grad_w_out1])[:, None],
    )


def solution(mesh):
    fine = Mesh(
        mesh.devices.reshape(mesh.shape["ea"], mesh.shape["row"] // 2, 2), ("ea", "half", "core")
    )
    row = ("half", "core")
    every = ("ea",) + row
    in_specs = (
        P(every, None),
        P(every, None),
        P(None, every, None),
        P(None, None, "ea"),
        P(None, None, "ea"),
        P(None, "ea", None),
        P(None, "ea", None),
        P(None, "ea", None),
        P(None, "ea", None, row),
        P(None, "ea", row, None),
    )
    out_specs = (
        P(every, None),
        P(every, None),
        P(None, None, "ea"),
        P(None, None, "ea"),
        P(None, "ea", None),
        P(None, "ea", None),
        P(None, "ea", None),
        P(None, "ea", None, row),
        P(None, "ea", row, None),
    )
    return jax.shard_map(
        per_device, mesh=fine, in_specs=in_specs, out_specs=out_specs, check_vma=False
    )
```

```python
import functools

import jax
import jax.numpy as jnp
from jax import lax
from jax.experimental import pallas as pl
from jax.experimental.pallas import tpu as pltpu
from jax.sharding import Mesh
from jax.sharding import PartitionSpec as P

HEADS = 12
HEAD = 64
SEQ = 197
LAYERS = 2
EPS = 1e-06
HIGH = lax.Precision.HIGHEST
BF = jnp.bfloat16
F32 = jnp.float32
SLOTS = 16
SCALE = HEAD ** (-0.5)
GROUP = ("ea", "half")
VMEM = 28 * 1024 * 1024


def dot(a, b, dims=((1,), (0,))):
    return lax.dot_general(a, b, (dims, ((), ())), preferred_element_type=F32)


def dot_nt(a, b):
    return dot(a, b, ((1,), (1,)))


def dot_tn(a, b):
    return dot(a, b, ((0,), (0,)))


def swap_core(value):
    return lax.ppermute(value, "core", [(0, 1), (1, 0)])


def exchange(rows):
    return lax.all_to_all(rows, GROUP, split_axis=0, concat_axis=0, tiled=True)


def gelu_parts(x):
    base = 1.0 + (0.3275911 * 0.7071067811865476) * jnp.abs(x)
    t = pl.reciprocal(base, approx=True)
    t = t * (2.0 - base * t)
    bell = jnp.exp2((x * x) * (-0.5 * 1.4426950408889634))
    poly = t * (
        0.5 * 0.254829592
        + t
        * (
            0.5 * -0.284496736
            + t * (0.5 * 1.421413741 + t * (0.5 * -1.453152027 + t * (0.5 * 1.061405429)))
        )
    )
    tail = poly * bell
    cdf = jnp.where(x < 0, tail, 1.0 - tail)
    return cdf, cdf + x * (bell * 0.3989422804014327)


def normalize(x, gain, bias):
    center = jnp.mean(x, axis=-1, keepdims=True)
    shifted = x - center
    spread = jnp.mean(shifted * shifted, axis=-1, keepdims=True)
    inv = lax.rsqrt(spread + EPS)
    unit = shifted * inv
    return unit * gain + bias, unit, inv


def normalize_back(grad, unit, inv, gain):
    scaled = grad * gain
    mean_a = jnp.mean(scaled, axis=-1, keepdims=True)
    mean_b = jnp.mean(scaled * unit, axis=-1, keepdims=True)
    return (
        inv * (scaled - mean_a - unit * mean_b),
        jnp.sum(grad * unit, axis=0),
        jnp.sum(grad, axis=0),
    )


def heads_of(matrix):
    return matrix.reshape(SEQ, HEADS, HEAD)


def copies(mine):
    return jnp.broadcast_to(mine[None], (lax.axis_size("ea"),) + mine.shape)


def gather_cols(sent):
    got = lax.all_to_all(sent, "ea", split_axis=0, concat_axis=0)
    return got.reshape(-1, sent.shape[2])


def core_half(value, which=0):
    n = value.shape[1] // 2
    core = lax.axis_index("core")
    return lax.dynamic_slice_in_dim(value, (core if which == 0 else 1 - core) * n, n, 1)


def in_order(own, other):
    first = lax.axis_index("core") == 0
    return jnp.concatenate(
        [jnp.where(first, own, other), jnp.where(first, other, own)], axis=1
    )


def thirds(value):
    n = value.shape[1] // 3
    return [value[:, i * n : (i + 1) * n] for i in range(3)]


def core_dense(qkv, out, small):
    return jnp.concatenate([core_half(part) for part in thirds(qkv)] + [core_half(out), small], axis=1)


def split_dense(own):
    return own, swap_core(own)


def sum_send(own, give):
    return (own.astype(F32) + swap_core(give).astype(F32)).astype(BF)


def sum_exchange(pair):
    groups = lax.axis_size("ea")
    return lax.all_to_all(
        pair.reshape(groups, -1, pair.shape[1]), "ea", split_axis=0, concat_axis=0
    )


def swap_row(value, flip):
    return lax.ppermute(value, ("half", "core"), [(i, i ^ flip) for i in range(4)])


def sum_finish(*parts):
    blocks = len(parts)
    part = jnp.concatenate([jnp.sum(p.astype(F32), axis=0) for p in parts], axis=0).astype(BF)
    full = part.astype(F32) + swap_row(part, 2).astype(F32)
    dense = part[:, :1536]
    other = swap_row(dense, 1).astype(F32) + swap_row(dense, 3).astype(F32)
    qkv = [
        in_order(own, more) for own, more in zip(thirds(full[:, :1152]), thirds(other[:, :1152]))
    ]
    return [
        value.reshape(blocks, -1, value.shape[1])
        for value in (
            jnp.concatenate(qkv, axis=1),
            in_order(full[:, 1152:1536], other[:, 1152:]),
            full[:, 1536:],
        )
    ]


def pad_cols(value, cols):
    return jnp.pad(value, ((0, 0), (0, cols - value.shape[1])))


def softmax_rows(scores):
    expo = jnp.exp(scores - jnp.max(scores, axis=-1, keepdims=True))
    return expo * (1.0 / jnp.sum(expo, axis=-1, keepdims=True))


def place(core, side, start, size):
    half = core if side == 0 else 1 - core
    return pl.ds(pl.multiple_of(half * 384 + start, 128), size)


def masked(pair, j):
    lane = lax.broadcasted_iota(jnp.int32, pair.shape, 1)
    return jnp.where((lane < HEAD) == (j == 0), pair, jnp.zeros_like(pair))


def merge(first, second):
    lane = lax.broadcasted_iota(jnp.int32, first.shape, 1)
    return jnp.where(lane < HEAD, first, second)


QKV = slice(0, 1152)
OUT = slice(1152, 1536)
SMALL = slice(1536, 1664)


def norms_of(own, experts):
    return own[:, SMALL].astype(F32).T[experts : experts + 4]


def attend_kernel(
    experts, core_ref, state, own, other, proj_o, proj_x, mixed, after, normed_two, logits, normed
):
    core = core_ref[0]
    norms = norms_of(own, experts)
    wide, _, _ = normalize(state[...], norms[0:1], norms[2:3])
    normed[...] = wide.astype(BF)
    for side, weight, proj in ((0, own, proj_o), (1, other, proj_x)):
        proj[...] = dot(normed[...], weight[:, QKV]).astype(BF)
        for at in range(0, 384, 128):
            query, key_part, value_part = (proj[:, i * 384 + at : i * 384 + at + 128] for i in range(3))
            found = []
            for j in range(2):
                shares = softmax_rows(dot_nt(masked(query, j), key_part) * SCALE)
                found.append(dot(shares.astype(BF), value_part))
            mixed[:, place(core, side, at, 128)] = merge(*found).astype(BF)
    for side, weight in ((0, own), (1, other)):
        cols = place(core, side, 0, 384)
        after[:, cols] = state[:, cols] + dot(mixed[...], weight[:, OUT])
    wide, _, _ = normalize(after[...], norms[1:2], norms[3:4])
    normed_two[...] = wide.astype(BF)
    logits[...] = dot(normed_two[...], own[:, SMALL])


def attend_back_kernel(
    experts, core_ref, grad, grad_two, state, after, proj_o, proj_x, mixed, small, own, other,
    grad_in, sum_o, sum_x, grad_attn, grad_mixed, gp_o, gp_x, normed, stats,
):
    core = core_ref[0]
    norms = norms_of(own, experts)
    _, unit, inv = normalize(after[...], norms[1:2], norms[3:4])
    part, gain_two, bias_two = normalize_back(grad_two[...], unit, inv, norms[1:2])
    grad_in[...] = grad[...] + part
    grad_attn[...] = grad_in[...].astype(BF)
    grad_mixed[...] = sum(
        dot_nt(grad_attn[:, place(core, side, 0, 384)], weight[:, OUT])
        for side, weight in ((0, own), (1, other))
    ).astype(BF)
    for side, proj, gp in ((0, proj_o, gp_o), (1, proj_x, gp_x)):
        for at in range(0, 384, 128):
            query, key_part, value_part = (proj[:, i * 384 + at : i * 384 + at + 128] for i in range(3))
            outer = grad_mixed[:, place(core, side, at, 128)]
            found = []
            for j in range(2):
                shares = softmax_rows(dot_nt(masked(query, j), key_part) * SCALE)
                grad_shares = dot_nt(masked(outer, j), value_part)
                inner = jnp.sum(grad_shares * shares, axis=-1, keepdims=True)
                raw = (shares * (grad_shares - inner) * SCALE).astype(BF)
                found.append(
                    (dot(raw, key_part), dot_tn(raw, query), dot_tn(shares.astype(BF), outer))
                )
            for i in range(3):
                gp[:, i * 384 + at : i * 384 + at + 128] = merge(found[0][i], found[1][i]).astype(BF)
    grad_normed = dot_nt(gp_o[...], own[:, QKV]) + dot_nt(gp_x[...], other[:, QKV])
    wide, unit, inv = normalize(state[...], norms[0:1], norms[2:3])
    normed[...] = wide.astype(BF)
    part, gain_one, bias_one = normalize_back(grad_normed, unit, inv, norms[0:1])
    grad_in[...] = grad_in[...] + part
    stats[...] = jnp.zeros_like(stats)
    for i, row in enumerate((gain_one, gain_two, bias_one, bias_two)):
        stats[experts + i : experts + i + 1, :] = row[None, :]
    narrow = (stats[...].T + small[...]).astype(BF)
    for side, gp, out in ((1, gp_x, sum_x), (0, gp_o, sum_o)):
        for at in range(0, 768, 256):
            rows = slice(at, at + 256)
            out[rows, QKV] = dot_tn(normed[:, rows], gp[...]).astype(BF)
            out[rows, OUT] = dot_tn(mixed[:, rows], grad_attn[:, place(core, side, 0, 384)]).astype(BF)
        out[:, SMALL] = narrow


def whole_call(kernel, args, outs, flops, scratch=()):
    core = lax.axis_index("core").astype(jnp.int32).reshape(1)
    vmem = pl.BlockSpec(memory_space=pltpu.VMEM)
    return pl.pallas_call(
        kernel,
        in_specs=[pl.BlockSpec(memory_space=pltpu.SMEM)] + [vmem] * len(args),
        out_specs=[vmem] * len(outs),
        out_shape=[jax.ShapeDtypeStruct(shape, kind) for shape, kind in outs],
        scratch_shapes=list(scratch),
        compiler_params=pltpu.CompilerParams(vmem_limit_bytes=VMEM + (12 << 20)),
        cost_estimate=pl.CostEstimate(flops=flops, bytes_accessed=8 << 20, transcendentals=0),
    )(core, *args)


def attention(state, dense):
    tokens, width = state.shape
    rows = lambda n, kind: ((tokens, n), kind)
    proj_o, proj_x, mixed, after, normed_two, logits = whole_call(
        functools.partial(attend_kernel, lax.axis_size("ea")),
        [state, *dense],
        [
            rows(1152, BF), rows(1152, BF), rows(width, BF), rows(width, F32), rows(width, BF),
            rows(128, F32),
        ],
        4 * tokens * width * (4 * width + 4 * tokens),
        [pltpu.VMEM((tokens, width), BF)],
    )
    return after, normed_two, logits, (state, proj_o, proj_x, mixed, after)


def attention_back(grad, grad_two, grad_router_w, kept, dense):
    state, proj_o, proj_x, mixed, after = kept
    tokens, width = grad.shape
    rows = lambda n, kind: ((tokens, n), kind)
    scratch = [rows(width, BF), rows(width, BF), rows(1152, BF), rows(1152, BF), rows(width, BF)]
    grad_in, sum_o, sum_x = whole_call(
        functools.partial(attend_back_kernel, lax.axis_size("ea")),
        [grad, grad_two, state, after, proj_o, proj_x, mixed, pad_cols(grad_router_w, 128), *dense],
        [rows(width, F32), ((width, 1664), BF), ((width, 1664), BF)],
        12 * tokens * width * (4 * width + 8 * tokens),
        [pltpu.VMEM(*dims) for dims in scratch + [((128, width), F32)]],
    )
    return grad_in, (sum_o, sum_x)


def forward_kernel(rows, w_in, w_out, hidden, slope, part):
    pre = dot(rows[...], w_in[0, 0])
    cdf, steep = gelu_parts(pre)
    hidden[...] = (pre * cdf).astype(BF)
    slope[...] = steep.astype(BF)
    part[...] = dot(hidden[...], w_out[0, 0]).astype(BF)


def backward_kernel(grows, slope, w_in, w_out, grad_pre, part):
    grad_hidden = dot_nt(grows[...], w_out[0, 0])
    grad_pre[...] = (grad_hidden * slope[...].astype(F32)).astype(BF)
    part[...] = dot_nt(grad_pre[...], w_in[0, 0]).astype(BF)


def both_kernel(rows, w_in, w_out, hidden, grad_pre, part):
    groups, _, slots, width = rows.shape
    pre = dot(rows[:, 0].reshape(groups * slots, width), w_in[0, 0])
    cdf, steep = gelu_parts(pre)
    hidden[...] = (pre * cdf).astype(BF)
    out = dot(hidden[...], w_out[0, 0]).astype(BF)
    part[:, 0] = out.reshape(groups, slots, width)
    grad_hidden = dot_nt(rows[:, 1].reshape(groups * slots, width), w_out[0, 0])
    grad_pre[...] = (grad_hidden * steep).astype(BF)
    out = dot_nt(grad_pre[...], w_in[0, 0]).astype(BF)
    part[:, 1] = out.reshape(groups, slots, width)


GROUPS = 32


def expert_call(kernel, depth, row_args, weights, out_dims, products):
    def spec(shape):
        block = (GROUPS * SLOTS,) + shape[1:] if len(shape) == 2 else (GROUPS,) + shape[1:]
        return pl.BlockSpec(block, lambda i: (i,) + (0,) * (len(shape) - 1))

    hidden_units, width = weights[1].shape[2:]
    count = row_args[-1].shape[0] * (1 if row_args[-1].ndim == 2 else SLOTS)
    moved = count * width * (len(row_args) + len(out_dims)) + 2 * hidden_units * width
    return pl.pallas_call(
        kernel,
        grid=(count // (GROUPS * SLOTS),),
        in_specs=[spec(a.shape) for a in row_args]
        + [pl.BlockSpec((1,) + w.shape[1:], lambda i: (depth, 0, 0, 0)) for w in weights],
        out_specs=[spec(shape) for shape in out_dims],
        out_shape=[jax.ShapeDtypeStruct(shape, BF) for shape in out_dims],
        compiler_params=pltpu.CompilerParams(vmem_limit_bytes=VMEM),
        cost_estimate=pl.CostEstimate(
            flops=2 * count * hidden_units * width * products,
            bytes_accessed=2 * moved,
            transcendentals=0,
        ),
    )(*row_args, *weights)


def join_cores(part_own, part_other):
    return (part_own.astype(F32) + swap_core(part_other).astype(F32)).astype(BF)


def routing(chosen, experts):
    flat = jnp.concatenate([chosen[:, 0], chosen[:, 1]])
    onehot = flat[:, None] == jnp.arange(experts, dtype=jnp.int32)[None, :]
    pairs = flat.shape[0]
    earlier = (
        lax.broadcasted_iota(jnp.int32, (pairs, pairs), 1)
        < lax.broadcasted_iota(jnp.int32, (pairs, pairs), 0)
    ).astype(BF)
    onehot = onehot.astype(F32)
    before = dot(earlier, onehot.astype(BF))
    position = jnp.sum(before * onehot, axis=1).astype(jnp.int32)
    return onehot, flat * SLOTS + position


def slot_codes(slots, kinds, dims, axis):
    row = lax.broadcasted_iota(jnp.int32, dims, axis)
    run = row // SLOTS
    return lax.rem(run, kinds), (run // (2 * kinds)) * SLOTS + lax.rem(row, SLOTS)


def one_hots(code, slots, kinds, kind):
    pairs = code.shape[0]
    found = []
    for dims, axis, codes in (((slots, pairs), 0, code[None, :]), ((pairs, slots), 1, code[:, None])):
        kind_of, slot_of = slot_codes(slots, kinds, dims, axis)
        found.append(((slot_of == codes) & (kind_of == kind)).astype(BF))
    return found


def router_forward(logits, onehot):
    router = jax.nn.softmax(logits, axis=-1)
    tokens = router.shape[0]
    gate = [
        jnp.sum(onehot[j * tokens : (j + 1) * tokens] * router, axis=1, keepdims=True)
        for j in range(2)
    ]
    return router, gate


def router_back(grad, picked, router, onehot, normed_two, router_w):
    tokens = router.shape[0]
    grad_router = 0.0
    for j in range(2):
        part = jnp.sum(grad * picked[j], axis=1, keepdims=True)
        grad_router = grad_router + onehot[j * tokens : (j + 1) * tokens] * part
    grad_logit = router * (grad_router - jnp.sum(grad_router * router, axis=-1, keepdims=True))
    grad_normed = jnp.dot(grad_logit, router_w.astype(F32).T, precision=HIGH)
    grad_router_w = jnp.dot(normed_two.astype(F32).T, grad_logit, precision=HIGH)
    return grad_normed, grad_router_w


def per_device(
    image_tokens,
    cotangent,
    routes,
    norm_gains,
    norm_biases,
    qkv_weight,
    out_weight,
    router_weight,
    expert_in,
    expert_out,
):
    tokens, width = image_tokens.shape
    experts = lax.axis_size("ea")
    mine = []
    for b in range(LAYERS):
        small = jnp.concatenate([router_weight[b], norm_gains[b].T, norm_biases[b].T], axis=1)
        mine.append(core_dense(qkv_weight[b], out_weight[b], pad_cols(small, 128)))
    gathered0, sent1 = lax.optimization_barrier((gather_cols(copies(mine[0])), copies(mine[1])))
    dense0 = split_dense(gathered0)
    weights = [expert_in, expert_out]
    onehot0, code = routing(routes[0], experts)
    send, fetch = one_hots(code, experts * 2 * SLOTS, 1, 0)
    onehot1, code = routing(routes[1], experts)
    send_rows, fetch_rows = one_hots(code, experts * 4 * SLOTS, 2, 0)
    send_grads, fetch_grads = one_hots(code, experts * 4 * SLOTS, 2, 1)
    send_rows = send_rows[:, :tokens] + send_rows[:, tokens:]
    fetch_grads = fetch_grads[:tokens] + fetch_grads[tokens:]
    send1 = jnp.concatenate([send_rows, send_grads], axis=1)
    fetch1 = jnp.concatenate([fetch_rows, fetch_grads], axis=0)

    state = image_tokens.astype(F32)
    after0, normed0, logits, kept0 = attention(state, dense0)
    router0, gate0 = router_forward(logits[:, :experts], onehot0)
    arrived = exchange(dot(send[:, :tokens] + send[:, tokens:], normed0).astype(BF))
    sent1, arrived = lax.optimization_barrier((sent1, arrived))
    gathered1 = gather_cols(sent1)
    rows0 = (arrived, swap_core(arrived))
    first = [
        expert_call(forward_kernel, 0, [r], weights, [r.shape] * 3, 2) for r in rows0
    ]
    hidden0, slope0, part = zip(*first)
    back, gathered1 = lax.optimization_barrier((join_cores(*part), gathered1))
    returned = exchange(back)
    dense1 = split_dense(gathered1)
    picked = dot(fetch, returned)
    picked0 = (picked[:tokens], picked[tokens:])
    state1 = after0 + gate0[0] * picked0[0] + gate0[1] * picked0[1]

    grad = cotangent.astype(F32)
    after1, normed1, logits, kept1 = attention(state1, dense1)
    router1, gate1 = router_forward(logits[:, :experts], onehot1)
    rows = jnp.concatenate([normed1] + [(g * grad).astype(BF) for g in gate1], axis=0)
    arrived = exchange(dot(send1, rows).astype(BF)).reshape(-1, 2, SLOTS, width)
    both = (arrived, swap_core(arrived))
    flat = (arrived.shape[0] * SLOTS, width)
    second = [
        expert_call(both_kernel, 1, [r], weights, [flat, flat, r.shape], 4) for r in both
    ]
    hidden1, grad_pre1, part = zip(*second)
    returned = exchange(join_cores(*part).reshape(-1, width))
    grad_w_out1 = sum(dot_tn(h, r[:, 1].reshape(flat)) for h, r in zip(hidden1, both))
    grad_w_in1 = sum(dot_tn(r[:, 0].reshape(flat), g) for r, g in zip(both, grad_pre1))
    returned, grad_w_out1, grad_w_in1 = lax.optimization_barrier(
        (returned, grad_w_out1, grad_w_in1)
    )
    picked = dot(fetch1, returned)
    picked1 = (picked[:tokens], picked[tokens : 2 * tokens])
    grad_sent = picked[2 * tokens :]
    block_out = (after1 + gate1[0] * picked1[0] + gate1[1] * picked1[1]).astype(BF)

    extra, grad_router_w1 = router_back(
        grad, picked1, router1, onehot1, normed1, dense1[0][:, 1536 : 1536 + experts]
    )
    grad, grads1 = attention_back(grad, grad_sent + extra, grad_router_w1, kept1, dense1)

    grad_rows = jnp.concatenate([(g * grad).astype(BF) for g in gate0], axis=0)
    arrived = exchange(dot(send, grad_rows).astype(BF))
    pair1 = sum_send(*grads1)
    arrived, pair1 = lax.optimization_barrier((arrived, pair1))
    grows0 = (arrived, swap_core(arrived))
    third = [
        expert_call(backward_kernel, 0, [r, s], weights, [r.shape] * 2, 2)
        for r, s in zip(grows0, slope0)
    ]
    grad_pre0, part = zip(*third)
    returned = exchange(join_cores(*part))
    grad_w_out0 = sum(dot_tn(h, g) for h, g in zip(hidden0, grows0))
    grad_w_in0 = sum(dot_tn(r, g) for r, g in zip(rows0, grad_pre0))
    returned, pair1, grad_w_out0, grad_w_in0 = lax.optimization_barrier(
        (returned, pair1, grad_w_out0, grad_w_in0)
    )
    parts1 = sum_exchange(pair1)
    picked = dot(fetch, returned)
    grad_sent = picked[:tokens] + picked[tokens:]
    extra, grad_router_w0 = router_back(
        grad, picked0, router0, onehot0, normed0, dense0[0][:, 1536 : 1536 + experts]
    )
    grad, grads0 = attention_back(grad, grad_sent + extra, grad_router_w0, kept0, dense0)
    grads0, parts1 = lax.optimization_barrier((grads0, parts1))
    parts0 = sum_exchange(sum_send(*grads0))
    qkv_sum, out_sum, small = sum_finish(parts0, parts1)

    return (
        block_out,
        grad,
        small[:, :, experts : experts + 2].transpose(0, 2, 1),
        small[:, :, experts + 2 : experts + 4].transpose(0, 2, 1),
        qkv_sum,
        out_sum,
        small[:, :, :experts],
        jnp.stack([grad_w_in0, grad_w_in1])[:, None],
        jnp.stack([grad_w_out0, grad_w_out1])[:, None],
    )


def solution(mesh):
    fine = Mesh(
        mesh.devices.reshape(mesh.shape["ea"], mesh.shape["row"] // 2, 2), ("ea", "half", "core")
    )
    row = ("half", "core")
    every = ("ea",) + row
    in_specs = (
        P(every, None),
        P(every, None),
        P(None, every, None),
        P(None, None, "ea"),
        P(None, None, "ea"),
        P(None, "ea", None),
        P(None, "ea", None),
        P(None, "ea", None),
        P(None, "ea", None, row),
        P(None, "ea", row, None),
    )
    out_specs = (
        P(every, None),
        P(every, None),
        P(None, None, "ea"),
        P(None, None, "ea"),
        P(None, "ea", None),
        P(None, "ea", None),
        P(None, "ea", None),
        P(None, "ea", None, row),
        P(None, "ea", row, None),
    )
    return jax.shard_map(
        per_device, mesh=fine, in_specs=in_specs, out_specs=out_specs, check_vma=False
    )
```
